256 devices in a mesh: seq: 32 (over y, x, core), head: 8 (over z).
Axes of the slice: x: 4, y: 4, z: 8, core: 2. Of those that a mesh axis runs over, the one named last changes fastest.
Arguments:
- queries: bfloat16 [32768, 4096], P('seq', 'head'), may hold values from -6 to 6
- keys: bfloat16 [32768, 4096], P('seq', 'head'), may hold values from -6 to 6
- values: bfloat16 [32768, 4096], P('seq', 'head'), may hold values from -6 to 6
- out_grad: bfloat16 [32768, 4096], P('seq', 'head'), may hold values from -6 to 6
- out_weight: bfloat16 [4096, 4096], P('head'), may hold values from -0.125 to 0.125
Outputs:
- query_gradient: bfloat16 [32768, 4096], P('seq', 'head')
- key_grad: bfloat16 [32768, 4096], P('seq', 'head')
- value_grad: bfloat16 [32768, 4096], P('seq', 'head')
The draws below stay inside these ranges and needn't reach their ends.
All inputs are finite; a program needn't handle non-finite values.
Results may differ from the reference program's by a relative error of at most 0.014.
Values may be sent and summed in bfloat16 or wider, within the bound.
A program may use at most 192 MiB of HBM per device.

```python
import math
import jax
import jax.numpy as jnp
from jax import lax

D = 4096
H = 32
HD = 128
TOK_DEV = 1024
LENGTH = 32768


def with_spikes(entries, stream_key, source, target, parts, factor):
    owner, partner = [(jnp.arange(entries.shape[position]) // (entries.shape[position] // parts)).reshape([-1 if axis == position else 1 for axis in range(entries.ndim)]) for position in (source, target)]
    chosen = jax.random.permutation(stream_key, parts)[partner]
    strong = (owner == chosen) | (owner == (partner + parts // 2) % parts)
    return jnp.where(strong, factor * entries, entries)


def level_of(key, dims, shards, smallest, largest):
    def one(dim, blocks):
        draws = jax.random.uniform(jax.random.fold_in(jax.random.fold_in(key, 6), dim), (blocks,), jnp.float32, smallest / len(shards), largest / len(shards))
        return jnp.repeat(jnp.exp(draws), dims[dim] // blocks).reshape((-1,) + (1,) * (len(dims) - dim - 1))

    level = one(*shards[0])
    for cut in shards[1:]:
        level = level * one(*cut)
    return level


def normal_values(stream_key, dims, width, most, cuts=(), kind=jnp.bfloat16):
    factor_of = level_of(stream_key, dims, cuts, -0.22, 0.18) if cuts else 1.0
    values = jax.random.normal(stream_key, dims, jnp.float32) * width * factor_of
    return jnp.minimum(jnp.maximum(values, -most), most).astype(kind)


def heavy_noise(key, extent, scale, most, shards, heavy, held_as=jnp.bfloat16):
    entries = scale * jax.random.normal(key, extent, jnp.float32)
    if shards:
        entries = entries * level_of(key, extent, shards, -0.22, 0.18)
    return jnp.clip(with_spikes(entries, jax.random.fold_in(key, 3), *heavy), -most, most).astype(held_as)


def setup_inputs(seed: int = 0) -> dict:
    splits = jax.random.split(jax.random.key(seed), 6)
    queries = normal_values(splits[0], (LENGTH, D), 1.0, 6.0, ((0, 32), (1, 8)))
    keys = normal_values(splits[1], (LENGTH, D), 1.0, 6.0, ((0, 32), (1, 8)))
    values = normal_values(splits[2], (LENGTH, D), 1.0, 6.0, ((0, 32), (1, 8)))
    out_grad = normal_values(splits[3], (LENGTH, D), 1.0, 6.0, ((0, 32), (1, 8)))
    out_weight = heavy_noise(splits[4], (D, D), D ** -0.5, 0.125, ((0, 8),), (1, 0, 8, 2.0))
    return dict(queries=queries, keys=keys, values=values, out_grad=out_grad, out_weight=out_weight)


def reference(queries, keys, values, out_grad, out_weight):
    blocks = LENGTH // TOK_DEV
    factor = 1.0 / math.sqrt(HD * LENGTH)
    head_grad = jnp.dot(out_grad, out_weight.T, preferred_element_type=jnp.float32).astype(jnp.bfloat16)
    query_blocks = queries.reshape(blocks, TOK_DEV, H, HD)
    key_blocks = keys.reshape(blocks, TOK_DEV, H, HD)
    value_blocks = values.reshape(blocks, TOK_DEV, H, HD)
    grad_blocks = head_grad.reshape(blocks, TOK_DEV, H, HD)
    highest_precision = lax.Precision.HIGHEST

    def key_step(running, inputs):
        key_piece, value_piece = inputs
        carried_state = jnp.einsum('buq,bud->uqd', key_piece.astype(jnp.float32), value_piece.astype(jnp.float32), precision=highest_precision)
        return (running + carried_state, running.astype(jnp.bfloat16))

    def query_step(running, inputs):
        query_part, grad_part = inputs
        carried_state = jnp.einsum('thq,tho->hqo', query_part.astype(jnp.float32), grad_part.astype(jnp.float32), precision=highest_precision)
        return (running + carried_state, running.astype(jnp.bfloat16))
    zero_state = jnp.zeros((H, HD, HD), jnp.float32)
    unused_one, prefix_total = lax.scan(key_step, zero_state, (key_blocks, value_blocks))
    unused_two, suffix = lax.scan(query_step, zero_state, (query_blocks, grad_blocks), reverse=True)
    causal = jnp.arange(TOK_DEV)[:, None] >= jnp.arange(TOK_DEV)[None, :]

    def one_block(inputs):
        query_f, key_float, value_f, gradient_float, prefix_float, suffix_f = [a.astype(jnp.float32) for a in inputs]
        score_gradient = jnp.where(causal[None], jnp.einsum('tho,sho->hts', gradient_float, value_f, precision=highest_precision), 0.0)
        score_gradient = score_gradient.astype(jnp.bfloat16).astype(jnp.float32)
        attn_scores = jnp.where(causal[None], jnp.einsum('thk,shk->hts', query_f, key_float, precision=highest_precision), 0.0)
        attn_scores = attn_scores.astype(jnp.bfloat16).astype(jnp.float32)
        query_gradient = jnp.einsum('ryx,xrj->yrj', score_gradient, key_float, precision=highest_precision) + jnp.einsum('lmp,mgp->lmg', gradient_float, prefix_float, precision=highest_precision)
        key_grad = jnp.einsum('hts,thq->shq', score_gradient, query_f, precision=highest_precision) + jnp.einsum('sho,hqo->shq', value_f, suffix_f, precision=highest_precision)
        value_grad = jnp.einsum('hts,tho->sho', attn_scores, gradient_float, precision=highest_precision) + jnp.einsum('shq,hqo->sho', key_float, suffix_f, precision=highest_precision)
        return ((factor * query_gradient).astype(jnp.bfloat16), (factor * key_grad).astype(jnp.bfloat16), (factor * value_grad).astype(jnp.bfloat16))
    query_gradient, key_grad, value_grad = lax.map(one_block, (query_blocks, key_blocks, value_blocks, grad_blocks, prefix_total, suffix))
    return (query_gradient.reshape(LENGTH, D), key_grad.reshape(LENGTH, D), value_grad.reshape(LENGTH, D))
```

```python
import functools
import math

import jax
import jax.numpy as jnp
from jax import lax
from jax.experimental import pallas as pl
from jax.experimental.pallas import tpu as pltpu
from jax.sharding import PartitionSpec as P

HD = 128
CH = 128
LANES = 8
BF = jnp.bfloat16
F32 = jnp.float32
MESH = pl.DeviceIdType.MESH


def mm(a, b, dims):
    return lax.dot_general(a, b, (dims, ((), ())), preferred_element_type=F32)


NN = ((1,), (0,))
NT = ((1,), (1,))
TN = ((0,), (0,))


def kernel(
    factor, zs, rows_n, heads,
    q_hbm, k_hbm, v_hbm, x_hbm, w_hbm,
    qg_hbm, kg_hbm, vg_hbm,
    q, k, v, w, xbuf, g, qg, kacc, vacc, kst, qst, qst_b, kgb, vgb,
    pre, suf, in1, in2, tot, out3,
    load_sem, store_sem, zsend, zrecv, s1, r1, s2, r2, s3, r3,
):
    tok = q.shape[0]
    width = x_hbm.shape[1]
    half = width // 2
    chunks = tok // CH
    z = lax.axis_index("head")
    seq = lax.axis_index("seq")
    lane = lax.rem(seq, LANES)
    row = seq // LANES
    right = lax.rem(z + 1, zs)
    left = lax.rem(z + zs - 1, zs)
    hops = zs // 2

    def seq_of(r, e):
        return r * LANES + e

    loads = [
        pltpu.make_async_copy(x_hbm, xbuf.at[z], load_sem.at[0]),
        pltpu.make_async_copy(k_hbm, k, load_sem.at[1]),
        pltpu.make_async_copy(v_hbm, v, load_sem.at[2]),
        pltpu.make_async_copy(w_hbm, w, load_sem.at[3]),
        pltpu.make_async_copy(q_hbm, q, load_sem.at[4]),
    ]
    for c in loads:
        c.start()

    barrier = pltpu.get_barrier_semaphore()
    for n in (left, right):
        pl.semaphore_signal(barrier, inc=1, device_id={"head": n}, device_id_type=MESH)
    for d in range(1, LANES):
        pl.semaphore_signal(
            barrier, inc=1, device_id={"seq": seq_of(row, lax.rem(lane + d, LANES))}, device_id_type=MESH
        )
    for d in range(1, rows_n):
        pl.semaphore_signal(
            barrier, inc=1, device_id={"seq": seq_of(lax.rem(row + d, rows_n), lane)}, device_id_type=MESH
        )
    pl.semaphore_wait(barrier, 2 + (LANES - 1) + (rows_n - 1))

    def ring(c, h):
        rows = pl.ds(pl.multiple_of(c * CH, CH), CH)
        copies = []
        for way, (to, sign) in enumerate(((right, -1), (left, 1))):
            src = lax.rem(z + zs + sign * (h - 1), zs)
            if h < hops:
                piece = xbuf.at[src, rows, :]
            else:
                piece = xbuf.at[src, rows, pl.ds(way * half, half)]
            copies.append(
                pltpu.make_async_remote_copy(
                    src_ref=piece,
                    dst_ref=piece,
                    send_sem=zsend.at[way, h - 1, c],
                    recv_sem=zrecv.at[way, h - 1, c],
                    device_id={"head": to},
                    device_id_type=MESH,
                )
            )
        return copies

    def send(c, h):
        for cp in ring(c, h):
            cp.start()

    def arrived(c, h):
        for cp in ring(c, h):
            cp.wait_recv()

    sl = heads * HD // LANES

    def ex1(which, st, d):
        to = lax.rem(lane + d, LANES)
        return pltpu.make_async_remote_copy(
            src_ref=st.at[pl.ds(pl.multiple_of(to * sl, sl), sl), :],
            dst_ref=in1.at[which, lane],
            send_sem=s1.at[which, d],
            recv_sem=r1.at[which, d],
            device_id={"seq": seq_of(row, to)},
            device_id_type=MESH,
        )

    def ex2(which, d):
        return pltpu.make_async_remote_copy(
            src_ref=tot.at[which],
            dst_ref=in2.at[which, row],
            send_sem=s2.at[which, d],
            recv_sem=r2.at[which, d],
            device_id={"seq": seq_of(lax.rem(row + d, rows_n), lane)},
            device_id_type=MESH,
        )

    def ex3(which, fin, d):
        to = lax.rem(lane + d, LANES)
        return pltpu.make_async_remote_copy(
            src_ref=out3.at[which, to],
            dst_ref=fin.at[pl.ds(pl.multiple_of(lane * sl, sl), sl), :],
            send_sem=s3.at[which, d],
            recv_sem=r3.at[which, d],
            device_id={"seq": seq_of(row, to)},
            device_id_type=MESH,
        )

    def phase1(which, st):
        for d in range(1, LANES):
            ex1(which, st, d).start()
        in1[which, lane] = st[pl.ds(pl.multiple_of(lane * sl, sl), sl), :]

    def phase2(which, st):
        for d in range(1, LANES):
            ex1(which, st, d).wait_recv()
        total = in1[which, 0].astype(F32)
        for e in range(1, LANES):
            total = total + in1[which, e].astype(F32)
        tot[which] = total
        for d in range(1, rows_n):
            ex2(which, d).start()

    def phase3(which, fin):
        for d in range(1, rows_n):
            ex2(which, d).wait_recv()
        in2[which, row] = jnp.zeros((sl, HD), F32)
        run = jnp.zeros((sl, HD), F32)
        for r in range(rows_n):
            keep = (r < row) if which == 0 else (r > row)
            run = run + jnp.where(keep, in2[which, r], 0.0)
        for e in range(LANES) if which == 0 else reversed(range(LANES)):
            out3[which, e] = run.astype(BF)
            run = run + in1[which, e].astype(F32)
        for d in range(1, LANES):
            ex3(which, fin, d).start()
        fin[pl.ds(pl.multiple_of(lane * sl, sl), sl), :] = out3[which, lane]

    def phase4(which, fin):
        for d in range(1, LANES):
            ex3(which, fin, d).wait_recv()

    def col(h):
        return pl.ds(h * HD, HD)

    def make_g(c):
        rows = pl.ds(pl.multiple_of(c * CH, CH), CH)
        x = jnp.concatenate([xbuf[s, rows, :] for s in range(zs)], axis=1)
        g[rows, :] = mm(x, w[...], NT).astype(BF)
        for h in range(heads):
            qst[col(h), :] += mm(q[rows, col(h)], g[rows, col(h)], TN)

    def head_part(c, h):
        rows = pl.ds(pl.multiple_of(c * CH, CH), CH)
        gc, qc = g[rows, col(h)], q[rows, col(h)]
        kh, vh = k[:, col(h)], v[:, col(h)]
        t = c * CH + lax.broadcasted_iota(jnp.int32, (CH, tok), 0)
        s = lax.broadcasted_iota(jnp.int32, (CH, tok), 1)
        sc = jnp.where(t >= s, mm(gc, vh, NT), 0.0).astype(BF)
        t2 = c * CH + lax.broadcasted_iota(jnp.int32, (tok, CH), 1)
        s2_ = lax.broadcasted_iota(jnp.int32, (tok, CH), 0)
        keep = t2 >= s2_
        sct = jnp.where(keep, mm(vh, gc, NT), 0.0).astype(BF)
        at = jnp.where(keep, mm(kh, qc, NT), 0.0).astype(BF)
        out = mm(sc, kh, NN) + mm(gc, pre[col(h), :], NT)
        qg[rows, col(h)] = (factor * out).astype(BF)
        kacc[:, col(h)] += mm(sct, qc, NN)
        vacc[:, col(h)] += mm(at, gc, NN)

    loads[0].wait()
    send(0, 1)
    send(1, 1)
    loads[1].wait()
    loads[2].wait()
    for h in range(heads):
        kst[col(h), :] = mm(k[:, col(h)], v[:, col(h)], TN).astype(BF)
    phase1(0, kst)
    kacc[...] = jnp.zeros_like(kacc)
    vacc[...] = jnp.zeros_like(vacc)
    qst[...] = jnp.zeros_like(qst)
    loads[3].wait()
    loads[4].wait()
    for h in range(2, hops + 1):
        for j in range(2):
            arrived(j, h - 1)
            send(j, h)
        if h == 2:
            phase2(0, kst)
        if h == 3:
            phase3(0, pre)
        if h == 4:
            phase4(0, pre)

    def pair(p, carry):
        a, b = 2 * p, 2 * p + 1
        send(a, 1)
        send(b, 1)
        arrived(a - 2, hops)
        make_g(a - 2)
        for h in range(2, hops + 1):
            for j, c in enumerate((a, b)):
                arrived(c, h - 1)
                send(c, h)
                if h == 2:
                    if j == 0:
                        head_part(a - 2, 0)
                        head_part(a - 2, 1)
                    else:
                        head_part(a - 2, 2)
                        head_part(a - 2, 3)
                if h == 3:
                    if j == 0:
                        arrived(b - 2, hops)
                        make_g(b - 2)
                    else:
                        head_part(b - 2, 0)
                        head_part(b - 2, 1)
                if h == 4 and j == 0:
                    head_part(b - 2, 2)
                    head_part(b - 2, 3)
        return carry

    lax.fori_loop(1, chunks // 2, pair, 0)
    a, b = chunks - 2, chunks - 1
    arrived(a, hops)
    make_g(a)
    arrived(b, hops)
    make_g(b)
    qst_b[...] = qst[...].astype(BF)
    phase1(1, qst_b)
    for h in range(heads):
        head_part(a, h)
    phase2(1, qst_b)
    head_part(b, 0)
    head_part(b, 1)
    phase3(1, suf)
    head_part(b, 2)
    head_part(b, 3)
    store_q = pltpu.make_async_copy(qg, qg_hbm, store_sem.at[0])
    store_q.start()
    phase4(1, suf)
    for h in range(heads):
        sh = suf[col(h), :]
        kgb[:, col(h)] = (factor * (kacc[:, col(h)] + mm(v[:, col(h)], sh, NT))).astype(BF)
    store_k = pltpu.make_async_copy(kgb, kg_hbm, store_sem.at[1])
    store_k.start()
    for h in range(heads):
        sh = suf[col(h), :]
        vgb[:, col(h)] = (factor * (vacc[:, col(h)] + mm(k[:, col(h)], sh, NN))).astype(BF)
    store_v = pltpu.make_async_copy(vgb, vg_hbm, store_sem.at[2])
    store_v.start()

    def drain(c, carry):
        for h in range(1, hops + 1):
            for cp in ring(c, h):
                cp.wait_send()
        return carry

    lax.fori_loop(0, chunks, drain, 0)
    for which, st, fin in ((0, kst, pre), (1, qst_b, suf)):
        for d in range(1, LANES):
            ex1(which, st, d).wait_send()
            ex3(which, fin, d).wait_send()
        for d in range(1, rows_n):
            ex2(which, d).wait_send()
    store_q.wait()
    store_k.wait()
    store_v.wait()


def on_device(queries, keys, values, out_grad, out_weight):
    tok, width = queries.shape
    zs = lax.axis_size("head")
    seqs = lax.axis_size("seq")
    heads = width // HD
    rows_n = seqs // LANES
    chunks = tok // CH
    sl = heads * HD // LANES
    factor = 1.0 / math.sqrt(HD * tok * seqs)
    out = jax.ShapeDtypeStruct((tok, width), BF)
    dma = pltpu.SemaphoreType.DMA
    return pl.pallas_call(
        functools.partial(kernel, factor, zs, rows_n, heads),
        out_shape=(out, out, out),
        in_specs=[pl.BlockSpec(memory_space=pl.ANY)] * 5,
        out_specs=[pl.BlockSpec(memory_space=pl.ANY)] * 3,
        scratch_shapes=[
            pltpu.VMEM((tok, width), BF),
            pltpu.VMEM((tok, width), BF),
            pltpu.VMEM((tok, width), BF),
            pltpu.VMEM((width, width * zs), BF),
            pltpu.VMEM((zs, tok, width), BF),
            pltpu.VMEM((tok, width), BF),
            pltpu.VMEM((tok, width), BF),
            pltpu.VMEM((tok, width), F32),
            pltpu.VMEM((tok, width), F32),
            pltpu.VMEM((width, HD), BF),
            pltpu.VMEM((width, HD), F32),
            pltpu.VMEM((width, HD), BF),
            pltpu.VMEM((tok, width), BF),
            pltpu.VMEM((tok, width), BF),
            pltpu.VMEM((width, HD), BF),
            pltpu.VMEM((width, HD), BF),
            pltpu.VMEM((2, LANES, sl, HD), BF),
            pltpu.VMEM((2, rows_n, sl, HD), F32),
            pltpu.VMEM((2, sl, HD), F32),
            pltpu.VMEM((2, LANES, sl, HD), BF),
            dma((5,)),
            dma((3,)),
            dma((2, zs // 2, chunks)),
            dma((2, zs // 2, chunks)),
            dma((2, LANES)),
            dma((2, LANES)),
            dma((2, rows_n)),
            dma((2, rows_n)),
            dma((2, LANES)),
            dma((2, LANES)),
        ],
        compiler_params=pltpu.CompilerParams(
            collective_id=0, has_side_effects=True, vmem_limit_bytes=56 * 1024 * 1024
        ),
        cost_estimate=pl.CostEstimate(
            flops=2 * tok * width * width * zs + 12 * tok * tok * width,
            bytes_accessed=16 * 1024 * 1024,
            transcendentals=0,
        ),
    )(queries, keys, values, out_grad, out_weight)


def solution(mesh):
    placed = (
        P("seq", "head"),
        P("seq", "head"),
        P("seq", "head"),
        P("seq", "head"),
        P("head", None),
    )
    return jax.shard_map(
        on_device,
        mesh=mesh,
        in_specs=placed,
        out_specs=(P("seq", "head"), P("seq", "head"), P("seq", "head")),
        check_vma=False,
    )
```

```python
import functools
import math

import jax
import jax.numpy as jnp
from jax import lax
from jax.experimental import pallas as pl
from jax.experimental.pallas import tpu as pltpu
from jax.sharding import PartitionSpec as P

HD = 128
CH = 128
BLK = 256
LANES = 8
BF = jnp.bfloat16
F32 = jnp.float32
MESH = pl.DeviceIdType.MESH


def mm(a, b, dims):
    return lax.dot_general(a, b, (dims, ((), ())), preferred_element_type=F32)


NN = ((1,), (0,))
NT = ((1,), (1,))
TN = ((0,), (0,))


def kernel(
    factor, zs, rows_n, heads,
    q_hbm, k_hbm, v_hbm, x_hbm, w_hbm,
    qg, kg, vg,
    q, k, v, w, xbuf, g, kacc, vacc, kst, qst, qst_b,
    pre, suf, in1, in2, tot, out3,
    load_sem, zsend, zrecv, s1, r1, s2, r2, s3, r3,
):
    tok = q.shape[0]
    width = x_hbm.shape[1]
    half = width // 2
    chunks = tok // CH
    z = lax.axis_index("head")
    seq = lax.axis_index("seq")
    lane = lax.rem(seq, LANES)
    row = seq // LANES
    right = lax.rem(z + 1, zs)
    left = lax.rem(z + zs - 1, zs)
    hops = zs // 2

    def seq_of(r, e):
        return r * LANES + e

    loads = [
        pltpu.make_async_copy(x_hbm, xbuf.at[z], load_sem.at[0]),
        pltpu.make_async_copy(k_hbm, k, load_sem.at[1]),
        pltpu.make_async_copy(v_hbm, v, load_sem.at[2]),
        pltpu.make_async_copy(w_hbm, w, load_sem.at[3]),
        pltpu.make_async_copy(q_hbm, q, load_sem.at[4]),
    ]
    for c in loads:
        c.start()

    barrier = pltpu.get_barrier_semaphore()
    for n in (left, right):
        pl.semaphore_signal(barrier, inc=1, device_id={"head": n}, device_id_type=MESH)
    for d in range(1, LANES):
        pl.semaphore_signal(
            barrier, inc=1, device_id={"seq": seq_of(row, lax.rem(lane + d, LANES))}, device_id_type=MESH
        )
    for d in range(1, rows_n):
        pl.semaphore_signal(
            barrier, inc=1, device_id={"seq": seq_of(lax.rem(row + d, rows_n), lane)}, device_id_type=MESH
        )
    pl.semaphore_wait(barrier, 2 + (LANES - 1) + (rows_n - 1))

    def ring(c, h):
        rows = pl.ds(pl.multiple_of(c * CH, CH), CH)
        copies = []
        for way, (to, sign) in enumerate(((right, -1), (left, 1))):
            src = lax.rem(z + zs + sign * (h - 1), zs)
            if h < hops:
                piece = xbuf.at[src, rows, :]
            else:
                piece = xbuf.at[src, rows, pl.ds(way * half, half)]
            copies.append(
                pltpu.make_async_remote_copy(
                    src_ref=piece,
                    dst_ref=piece,
                    send_sem=zsend.at[way, h - 1, c],
                    recv_sem=zrecv.at[way, h - 1, c],
                    device_id={"head": to},
                    device_id_type=MESH,
                )
            )
        return copies

    def send(c, h):
        for cp in ring(c, h):
            cp.start()

    def arrived(c, h):
        for cp in ring(c, h):
            cp.wait_recv()

    sl = heads * HD // LANES

    def ex1(which, st, d):
        to = lax.rem(lane + d, LANES)
        return pltpu.make_async_remote_copy(
            src_ref=st.at[pl.ds(pl.multiple_of(to * sl, sl), sl), :],
            dst_ref=in1.at[which, lane],
            send_sem=s1.at[which, d],
            recv_sem=r1.at[which, d],
            device_id={"seq": seq_of(row, to)},
            device_id_type=MESH,
        )

    def ex2(which, d):
        return pltpu.make_async_remote_copy(
            src_ref=tot.at[which],
            dst_ref=in2.at[which, row],
            send_sem=s2.at[which, d],
            recv_sem=r2.at[which, d],
            device_id={"seq": seq_of(lax.rem(row + d, rows_n), lane)},
            device_id_type=MESH,
        )

    def ex3(which, fin, d):
        to = lax.rem(lane + d, LANES)
        return pltpu.make_async_remote_copy(
            src_ref=out3.at[which, to],
            dst_ref=fin.at[pl.ds(pl.multiple_of(lane * sl, sl), sl), :],
            send_sem=s3.at[which, d],
            recv_sem=r3.at[which, d],
            device_id={"seq": seq_of(row, to)},
            device_id_type=MESH,
        )

    def phase1(which, st):
        for d in range(1, LANES):
            ex1(which, st, d).start()
        in1[which, lane] = st[pl.ds(pl.multiple_of(lane * sl, sl), sl), :]

    def phase2(which, st):
        for d in range(1, LANES):
            ex1(which, st, d).wait_recv()
        total = in1[which, 0].astype(F32)
        for e in range(1, LANES):
            total = total + in1[which, e].astype(F32)
        tot[which] = total
        for d in range(1, rows_n):
            ex2(which, d).start()

    def phase3(which, fin):
        for d in range(1, rows_n):
            ex2(which, d).wait_recv()
        in2[which, row] = jnp.zeros((sl, HD), F32)
        run = jnp.zeros((sl, HD), F32)
        for r in range(rows_n):
            keep = (r < row) if which == 0 else (r > row)
            run = run + jnp.where(keep, in2[which, r], 0.0)
        for e in range(LANES) if which == 0 else reversed(range(LANES)):
            out3[which, e] = run.astype(BF)
            run = run + in1[which, e].astype(F32)
        for d in range(1, LANES):
            ex3(which, fin, d).start()
        fin[pl.ds(pl.multiple_of(lane * sl, sl), sl), :] = out3[which, lane]

    def phase4(which, fin):
        for d in range(1, LANES):
            ex3(which, fin, d).wait_recv()

    def col(h):
        return pl.ds(h * HD, HD)

    def make_g(t0):
        rows = pl.ds(t0, BLK)
        x = jnp.concatenate([xbuf[s, rows, :] for s in range(zs)], axis=1)
        g[rows, :] = mm(x, w[...], NT).astype(BF)
        for h in range(heads):
            qst[col(h), :] += mm(q[rows, col(h)], g[rows, col(h)], TN)

    def head_part(h, t0, t1):
        causal = lax.broadcasted_iota(jnp.int32, (BLK, BLK), 0) >= lax.broadcasted_iota(
            jnp.int32, (BLK, BLK), 1
        )
        causal_t = lax.broadcasted_iota(jnp.int32, (BLK, BLK), 1) >= lax.broadcasted_iota(
            jnp.int32, (BLK, BLK), 0
        )
        for s0 in range(0, t1, BLK):
            first = max(s0, t0)
            rows, here = pl.ds(first, t1 - first), pl.ds(s0, BLK)

            def masked(a, s0=s0):
                if s0 < t0:
                    return a.astype(BF)
                diag = jnp.where(causal_t, a[:, :BLK], 0.0)
                if a.shape[1] > BLK:
                    diag = jnp.concatenate([diag, a[:, BLK:]], axis=1)
                return diag.astype(BF)

            sct = masked(mm(v[here, col(h)], g[rows, col(h)], NT))
            at = masked(mm(k[here, col(h)], q[rows, col(h)], NT))
            kpart = mm(sct, q[rows, col(h)], NN)
            vpart = mm(at, g[rows, col(h)], NN)
            if s0 < t0:
                kpart = kpart + kacc[here, col(h)]
                vpart = vpart + vacc[here, col(h)]
            kacc[here, col(h)] = kpart
            vacc[here, col(h)] = vpart
        for r0 in range(t0, t1, BLK):
            rows, past = pl.ds(r0, BLK), pl.ds(0, r0 + BLK)
            a = mm(g[rows, col(h)], v[past, col(h)], NT)
            diag = jnp.where(causal, a[:, r0:], 0.0)
            if r0:
                diag = jnp.concatenate([a[:, :r0], diag], axis=1)
            out = mm(diag.astype(BF), k[past, col(h)], NN) + mm(g[rows, col(h)], pre[col(h), :], NT)
            qg[rows, col(h)] = (factor * out).astype(BF)

    depth = chunks // 2
    group = [(c, h) for h in range(1, hops + 1) for c in range(depth)]
    mid = tok // 2

    loads[0].wait()
    for c in range(depth):
        send(c, 1)
    loads[1].wait()
    loads[2].wait()
    for h in range(heads):
        kst[col(h), :] = mm(k[:, col(h)], v[:, col(h)], TN).astype(BF)
    phase1(0, kst)
    qst[...] = jnp.zeros_like(qst)
    loads[3].wait()
    loads[4].wait()
    for c, h in group[depth:]:
        arrived(c, h - 1)
        send(c, h)
        if c == depth - 1:
            if h == 2:
                phase2(0, kst)
            if h == 3:
                phase3(0, pre)
            if h == 4:
                phase4(0, pre)
    for c in range(depth):
        send(depth + c, 1)
    for c in range(depth):
        arrived(c, hops)
    work = []
    for t0 in range(0, mid, BLK):
        work.append(functools.partial(make_g, t0))
    for h in range(heads):
        work.append(functools.partial(head_part, h, 0, mid))
    for c, h in group[depth:]:
        arrived(depth + c, h - 1)
        send(depth + c, h)
        if work:
            work.pop(0)()
    for f in work:
        f()
    per = BLK // CH
    for i in range(depth // per):
        for c in range(i * per, (i + 1) * per):
            arrived(depth + c, hops)
        make_g(mid + i * BLK)
    qst_b[...] = qst[...].astype(BF)
    phase1(1, qst_b)
    for h in range(heads):
        head_part(h, mid, tok)
        if h == heads // 2 - 1:
            phase2(1, qst_b)
    phase3(1, suf)
    phase4(1, suf)
    for h in range(heads):
        sh = suf[col(h), :]
        kg[:, col(h)] = (factor * (kacc[:, col(h)] + mm(v[:, col(h)], sh, NT))).astype(BF)
        vg[:, col(h)] = (factor * (vacc[:, col(h)] + mm(k[:, col(h)], sh, NN))).astype(BF)

    def drain(c, carry):
        for h in range(1, hops + 1):
            for cp in ring(c, h):
                cp.wait_send()
        return carry

    lax.fori_loop(0, chunks, drain, 0)
    for which, st, fin in ((0, kst, pre), (1, qst_b, suf)):
        for d in range(1, LANES):
            ex1(which, st, d).wait_send()
            ex3(which, fin, d).wait_send()
        for d in range(1, rows_n):
            ex2(which, d).wait_send()


def on_device(queries, keys, values, out_grad, out_weight):
    tok, width = queries.shape
    zs = lax.axis_size("head")
    seqs = lax.axis_size("seq")
    heads = width // HD
    rows_n = seqs // LANES
    chunks = tok // CH
    sl = heads * HD // LANES
    factor = 1.0 / math.sqrt(HD * tok * seqs)
    out = pltpu.VMEM((tok, width), BF)
    dma = pltpu.SemaphoreType.DMA
    return pl.pallas_call(
        functools.partial(kernel, factor, zs, rows_n, heads),
        out_shape=(out, out, out),
        in_specs=[pl.BlockSpec(memory_space=pltpu.HBM)] * 5,
        out_specs=[pl.BlockSpec(memory_space=pltpu.VMEM)] * 3,
        scratch_shapes=[
            pltpu.VMEM((tok, width), BF),
            pltpu.VMEM((tok, width), BF),
            pltpu.VMEM((tok, width), BF),
            pltpu.VMEM((width, width * zs), BF),
            pltpu.VMEM((zs, tok, width), BF),
            pltpu.VMEM((tok, width), BF),
            pltpu.VMEM((tok, width), F32),
            pltpu.VMEM((tok, width), F32),
            pltpu.VMEM((width, HD), BF),
            pltpu.VMEM((width, HD), F32),
            pltpu.VMEM((width, HD), BF),
            pltpu.VMEM((width, HD), BF),
            pltpu.VMEM((width, HD), BF),
            pltpu.VMEM((2, LANES, sl, HD), BF),
            pltpu.VMEM((2, rows_n, sl, HD), F32),
            pltpu.VMEM((2, sl, HD), F32),
            pltpu.VMEM((2, LANES, sl, HD), BF),
            dma((5,)),
            dma((2, zs // 2, chunks)),
            dma((2, zs // 2, chunks)),
            dma((2, LANES)),
            dma((2, LANES)),
            dma((2, rows_n)),
            dma((2, rows_n)),
            dma((2, LANES)),
            dma((2, LANES)),
        ],
        compiler_params=pltpu.CompilerParams(
            collective_id=0, has_side_effects=True, vmem_limit_bytes=60 * 1024 * 1024
        ),
        cost_estimate=pl.CostEstimate(
            flops=2 * tok * width * width * zs + 12 * tok * tok * width,
            bytes_accessed=16 * 1024 * 1024,
            transcendentals=0,
        ),
    )(queries, keys, values, out_grad, out_weight)


def solution(mesh):
    placed = (
        P("seq", "head"),
        P("seq", "head"),
        P("seq", "head"),
        P("seq", "head"),
        P("head", None),
    )
    return jax.shard_map(
        on_device,
        mesh=mesh,
        in_specs=placed,
        out_specs=(P("seq", "head"), P("seq", "head"), P("seq", "head")),
        check_vma=False,
    )
```

```python
import functools
import math

import jax
import jax.numpy as jnp
from jax import lax
from jax.experimental import pallas as pl
from jax.experimental.pallas import tpu as pltpu
from jax.sharding import PartitionSpec as P

HD = 128
CH = 64
BLK = 256
LANES = 8
BF = jnp.bfloat16
F32 = jnp.float32
MESH = pl.DeviceIdType.MESH


def mm(a, b, dims):
    return lax.dot_general(a, b, (dims, ((), ())), preferred_element_type=F32)


NN = ((1,), (0,))
NT = ((1,), (1,))
TN = ((0,), (0,))


def kernel(
    factor, zs, rows_n, heads,
    q_hbm, k_hbm, v_hbm, x_hbm, w_hbm,
    qg, kg, vg,
    q, k, v, w, xown, xq, gout, g, kacc, vacc, kst, qst, qst_b,
    pre, suf, in1, in2, tot, out3,
    load_sem, zsend, zrecv, fsend, frecv, wsend, wrecv, asend, arecv, bsend, brecv, dsend, drecv, csend, crecv, osend, orecv, s1, r1, s2, r2, s3, r3,
):
    tok = q.shape[0]
    quarter = tok // 4
    subs = quarter // CH
    z = lax.axis_index("head")
    seq = lax.axis_index("seq")
    lane = lax.rem(seq, LANES)
    row = seq // LANES
    y, x, c = row, lane // 2, lax.rem(lane, 2)
    pair = z // 2
    side = 2 * lax.rem(z, 2) - 1

    def layer(n):
        return lax.rem(z + zs + n * side, zs)

    def seq_of(r, e):
        return r * LANES + e

    mine = pl.ds(pl.multiple_of(pair * quarter, quarter), quarter)
    loads = [
        pltpu.make_async_copy(x_hbm, xown, load_sem.at[0]),
        pltpu.make_async_copy(k_hbm, k, load_sem.at[1]),
        pltpu.make_async_copy(v_hbm, v, load_sem.at[2]),
        pltpu.make_async_copy(x_hbm.at[mine, :], xq.at[z], load_sem.at[3]),
        pltpu.make_async_copy(w_hbm, w.at[0], load_sem.at[4]),
        pltpu.make_async_copy(q_hbm, q, load_sem.at[5]),
    ]
    for cp in loads:
        cp.start()

    barrier = pltpu.get_barrier_semaphore()
    for n in (1, -1, 2, -2, 3):
        pl.semaphore_signal(barrier, inc=1, device_id={"head": layer(n)}, device_id_type=MESH)
    for d in range(1, LANES):
        pl.semaphore_signal(
            barrier, inc=1, device_id={"seq": seq_of(row, lax.rem(lane + d, LANES))}, device_id_type=MESH
        )
    for d in range(1, rows_n):
        pl.semaphore_signal(
            barrier, inc=1, device_id={"seq": seq_of(lax.rem(row + d, rows_n), lane)}, device_id_type=MESH
        )
    pl.semaphore_wait(barrier, 5 + (LANES - 1) + (rows_n - 1))

    def remote(ref, dst, send_sem, recv_sem, to):
        return pltpu.make_async_remote_copy(
            src_ref=ref, dst_ref=dst, send_sem=send_sem, recv_sem=recv_sem, device_id=to, device_id_type=MESH
        )

    def x_first(i, n):
        to = layer((1, -2, 3, -1)[i])
        rows = pl.ds(pl.multiple_of(to // 2 * quarter + n * CH, CH), CH)
        return remote(
            xown.at[rows, :], xq.at[z, pl.ds(n * CH, CH), :], zsend.at[i, n], zrecv.at[i, n], {"head": to}
        )

    def x_relay(i, n):
        piece = xq.at[layer(i + 1), pl.ds(n * CH, CH), :]
        return remote(piece, piece, fsend.at[i, n], frecv.at[i, n], {"head": layer(-1)})

    def w_z(b):
        return remote(
            w_hbm.at[y, x, c], w.at[b, y, x, c], wsend.at[b - 1], wrecv.at[b - 1], {"head": layer((1, -2, 3)[b - 1])}
        )

    half = x_hbm.shape[1] * zs // 2

    def w_first(b, part, d):
        piece = w.at[b, y, x, c, :, pl.ds(part * half, half)]
        to = seq_of(y, lax.rem(lane + 2 * d, LANES)) if part == 0 else seq_of(lax.rem(y + d, rows_n), lane)
        return remote(piece, piece, asend.at[b - 1, part, d - 1], arecv.at[b - 1, part, d - 1], {"seq": to})

    def w_line(b, part, n, cols):
        if part == 0:
            return w.at[b, lax.rem(y + n, rows_n), :, c, :, cols]
        return w.at[b, :, lax.rem(x + n, LANES // 2), c, :, cols]

    def w_next(part, n):
        if part == 0:
            return {"seq": seq_of(lax.rem(y + n, rows_n), lane)}
        return {"seq": seq_of(y, lax.rem(lane + 2 * n, LANES))}

    def w_second(b, part, way):
        piece = w_line(b, part, 0, pl.ds(part * half, half))
        return remote(
            piece, piece, bsend.at[b - 1, part, way], brecv.at[b - 1, part, way], w_next(part, (1, 3)[way])
        )

    def w_third(b, part, way):
        piece = w_line(b, part, (3, 1)[way], pl.ds(part * half + way * (half // 2), half // 2))
        return remote(
            piece, piece, dsend.at[b - 1, part, way], drecv.at[b - 1, part, way], w_next(part, (1, 3)[way])
        )

    def w_core(b):
        piece = w.at[b, :, :, c]
        return remote(piece, piece, csend.at[b - 1], crecv.at[b - 1], {"seq": seq_of(y, 2 * x + 1 - c)})

    def g_back(b):
        return remote(
            gout.at[b - 1], g.at[mine, :], osend.at[b - 1], orecv.at[b - 1], {"head": layer(b)}
        )

    ring3 = [(part, d) for part in range(2) for d in range(1, rows_n)]
    ways = [(part, way) for part in range(2) for way in range(2)]

    def start(make, b, keys):
        for key in keys:
            make(b, *key).start()

    def wait(make, b, keys):
        for key in keys:
            make(b, *key).wait_recv()

    def x_send(n):
        for i in (2, 1, 0, 3):
            x_first(i, n).start()

    def x_pass(n):
        for i in range(3):
            x_first(i, n).wait_recv()
            x_relay(i, n).start()

    sl = heads * HD // LANES

    def ex1(which, st, d):
        to = lax.rem(lane + d, LANES)
        return pltpu.make_async_remote_copy(
            src_ref=st.at[pl.ds(pl.multiple_of(to * sl, sl), sl), :],
            dst_ref=in1.at[which, lane],
            send_sem=s1.at[which, d],
            recv_sem=r1.at[which, d],
            device_id={"seq": seq_of(row, to)},
            device_id_type=MESH,
        )

    def ex2(which, d):
        return pltpu.make_async_remote_copy(
            src_ref=tot.at[which],
            dst_ref=in2.at[which, row],
            send_sem=s2.at[which, d],
            recv_sem=r2.at[which, d],
            device_id={"seq": seq_of(lax.rem(row + d, rows_n), lane)},
            device_id_type=MESH,
        )

    def ex3(which, fin, d):
        to = lax.rem(lane + d, LANES)
        return pltpu.make_async_remote_copy(
            src_ref=out3.at[which, to],
            dst_ref=fin.at[pl.ds(pl.multiple_of(lane * sl, sl), sl), :],
            send_sem=s3.at[which, d],
            recv_sem=r3.at[which, d],
            device_id={"seq": seq_of(row, to)},
            device_id_type=MESH,
        )

    def phase1(which, st):
        for d in range(1, LANES):
            ex1(which, st, d).start()
        in1[which, lane] = st[pl.ds(pl.multiple_of(lane * sl, sl), sl), :]

    def phase2(which, st):
        for d in range(1, LANES):
            ex1(which, st, d).wait_recv()
        total = in1[which, 0].astype(F32)
        for e in range(1, LANES):
            total = total + in1[which, e].astype(F32)
        tot[which] = total
        for d in range(1, rows_n):
            ex2(which, d).start()

    def phase3(which, fin):
        for d in range(1, rows_n):
            ex2(which, d).wait_recv()
        in2[which, row] = jnp.zeros((sl, HD), F32)
        run = jnp.zeros((sl, HD), F32)
        for r in range(rows_n):
            keep = (r < row) if which == 0 else (r > row)
            run = run + jnp.where(keep, in2[which, r], 0.0)
        for e in range(LANES) if which == 0 else reversed(range(LANES)):
            out3[which, e] = run.astype(BF)
            run = run + in1[which, e].astype(F32)
        for d in range(1, LANES):
            ex3(which, fin, d).start()
        fin[pl.ds(pl.multiple_of(lane * sl, sl), sl), :] = out3[which, lane]

    def phase4(which, fin):
        for d in range(1, LANES):
            ex3(which, fin, d).wait_recv()

    def col(h):
        return pl.ds(h * HD, HD)

    def product(b):
        xs = jnp.concatenate([xq[s] for s in range(zs)], axis=1)
        wb = w[b].reshape(x_hbm.shape[1], x_hbm.shape[1] * zs)
        return mm(xs, wb, NT).astype(BF)

    def add_state(rows):
        for h in range(heads):
            qst[col(h), :] += mm(q[rows, col(h)], g[rows, col(h)], TN)

    def head_part(h, t0, t1):
        causal = lax.broadcasted_iota(jnp.int32, (BLK, BLK), 0) >= lax.broadcasted_iota(
            jnp.int32, (BLK, BLK), 1
        )
        causal_t = lax.broadcasted_iota(jnp.int32, (BLK, BLK), 1) >= lax.broadcasted_iota(
            jnp.int32, (BLK, BLK), 0
        )
        for s0 in range(0, t1, BLK):
            first = max(s0, t0)
            rows, here = pl.ds(first, t1 - first), pl.ds(s0, BLK)

            def masked(a, s0=s0):
                if s0 < t0:
                    return a.astype(BF)
                diag = jnp.where(causal_t, a[:, :BLK], 0.0)
                if a.shape[1] > BLK:
                    diag = jnp.concatenate([diag, a[:, BLK:]], axis=1)
                return diag.astype(BF)

            sct = masked(mm(v[here, col(h)], g[rows, col(h)], NT))
            at = masked(mm(k[here, col(h)], q[rows, col(h)], NT))
            kpart = mm(sct, q[rows, col(h)], NN)
            vpart = mm(at, g[rows, col(h)], NN)
            if s0 < t0:
                kpart = kpart + kacc[here, col(h)]
                vpart = vpart + vacc[here, col(h)]
            kacc[here, col(h)] = kpart
            vacc[here, col(h)] = vpart
        for r0 in range(t0, t1, BLK):
            rows, past = pl.ds(r0, BLK), pl.ds(0, r0 + BLK)
            a = mm(g[rows, col(h)], v[past, col(h)], NT)
            diag = jnp.where(causal, a[:, r0:], 0.0)
            if r0:
                diag = jnp.concatenate([a[:, :r0], diag], axis=1)
            out = mm(diag.astype(BF), k[past, col(h)], NN) + mm(g[rows, col(h)], pre[col(h), :], NT)
            qg[rows, col(h)] = (factor * out).astype(BF)

    for b in (3, 2, 1):
        w_z(b).start()
    loads[0].wait()
    x_send(0)
    loads[1].wait()
    loads[2].wait()
    for h in range(heads):
        kst[col(h), :] = mm(k[:, col(h)], v[:, col(h)], TN).astype(BF)
    phase1(0, kst)
    qst[...] = jnp.zeros_like(qst)
    for b in (3, 2, 1):
        w_z(b).wait_recv()
        start(w_first, b, ring3)
        x_send(4 - b)
    wait(w_first, 3, ring3)
    start(w_second, 3, ways)
    x_pass(0)
    phase2(0, kst)
    wait(w_first, 2, ring3)
    wait(w_first, 1, ring3)
    x_pass(1)
    phase3(0, pre)
    wait(w_second, 3, ways)
    start(w_third, 3, ways)
    start(w_second, 2, ways)
    x_pass(2)
    phase4(0, pre)
    wait(w_third, 3, ways)
    w_core(3).start()
    wait(w_second, 2, ways)
    start(w_third, 2, ways)
    start(w_second, 1, ways)
    x_pass(3)
    for n in range(subs):
        x_first(3, n).wait_recv()
        for i in range(3):
            x_relay(i, n).wait_recv()
    for cp in loads[3:]:
        cp.wait()
    w_core(3).wait_recv()
    gout[2] = product(3)
    g_back(3).start()
    wait(w_third, 2, ways)
    w_core(2).start()
    wait(w_second, 1, ways)
    start(w_third, 1, ways)
    g[mine, :] = product(0)
    add_state(mine)
    w_core(2).wait_recv()
    gout[1] = product(2)
    g_back(2).start()
    wait(w_third, 1, ways)
    w_core(1).start()
    w_core(1).wait_recv()
    gout[0] = product(1)
    g_back(1).start()
    for b in (3, 2, 1):
        g_back(b).wait_recv()
        add_state(pl.ds(pl.multiple_of(layer((1, -2, 3)[b - 1]) // 2 * quarter, quarter), quarter))
    qst_b[...] = qst[...].astype(BF)
    phase1(1, qst_b)
    for h in range(heads):
        head_part(h, 0, tok)
        if h == 1:
            phase2(1, qst_b)
        if h == 2:
            phase3(1, suf)
    phase4(1, suf)
    for h in range(heads):
        sh = suf[col(h), :]
        kg[:, col(h)] = (factor * (kacc[:, col(h)] + mm(v[:, col(h)], sh, NT))).astype(BF)
        vg[:, col(h)] = (factor * (vacc[:, col(h)] + mm(k[:, col(h)], sh, NN))).astype(BF)

    for n in range(subs):
        for i in range(4):
            x_first(i, n).wait_send()
        for i in range(3):
            x_relay(i, n).wait_send()
    for b in range(1, 4):
        w_z(b).wait_send()
        for key in ring3:
            w_first(b, *key).wait_send()
        for key in ways:
            w_second(b, *key).wait_send()
            w_third(b, *key).wait_send()
        w_core(b).wait_send()
        g_back(b).wait_send()
    for which, st, fin in ((0, kst, pre), (1, qst_b, suf)):
        for d in range(1, LANES):
            ex1(which, st, d).wait_send()
            ex3(which, fin, d).wait_send()
        for d in range(1, rows_n):
            ex2(which, d).wait_send()


def on_device(queries, keys, values, out_grad, out_weight):
    tok, width = queries.shape
    zs = lax.axis_size("head")
    seqs = lax.axis_size("seq")
    heads = width // HD
    rows_n = seqs // LANES
    subs = tok // 4 // CH
    sl = heads * HD // LANES
    factor = 1.0 / math.sqrt(HD * tok * seqs)
    out = pltpu.VMEM((tok, width), BF)
    slices = out_weight.reshape(rows_n, LANES // 2, 2, width // seqs, width * zs)
    dma = pltpu.SemaphoreType.DMA
    return pl.pallas_call(
        functools.partial(kernel, factor, zs, rows_n, heads),
        out_shape=(out, out, out),
        in_specs=[pl.BlockSpec(memory_space=pltpu.HBM)] * 5,
        out_specs=[pl.BlockSpec(memory_space=pltpu.VMEM)] * 3,
        scratch_shapes=[
            pltpu.VMEM((tok, width), BF),
            pltpu.VMEM((tok, width), BF),
            pltpu.VMEM((tok, width), BF),
            pltpu.VMEM((4, rows_n, LANES // 2, 2, width // seqs, width * zs), BF),
            pltpu.VMEM((tok, width), BF),
            pltpu.VMEM((zs, tok // 4, width), BF),
            pltpu.VMEM((3, tok // 4, width), BF),
            pltpu.VMEM((tok, width), BF),
            pltpu.VMEM((tok, width), F32),
            pltpu.VMEM((tok, width), F32),
            pltpu.VMEM((width, HD), BF),
            pltpu.VMEM((width, HD), F32),
            pltpu.VMEM((width, HD), BF),
            pltpu.VMEM((width, HD), BF),
            pltpu.VMEM((width, HD), BF),
            pltpu.VMEM((2, LANES, sl, HD), BF),
            pltpu.VMEM((2, rows_n, sl, HD), F32),
            pltpu.VMEM((2, sl, HD), F32),
            pltpu.VMEM((2, LANES, sl, HD), BF),
            dma((6,)),
            dma((4, subs)),
            dma((4, subs)),
            dma((3, subs)),
            dma((3, subs)),
            dma((3,)),
            dma((3,)),
            dma((3, 2, rows_n - 1)),
            dma((3, 2, rows_n - 1)),
            dma((3, 2, 2)),
            dma((3, 2, 2)),
            dma((3, 2, 2)),
            dma((3, 2, 2)),
            dma((3,)),
            dma((3,)),
            dma((3,)),
            dma((3,)),
            dma((2, LANES)),
            dma((2, LANES)),
            dma((2, rows_n)),
            dma((2, rows_n)),
            dma((2, LANES)),
            dma((2, LANES)),
        ],
        compiler_params=pltpu.CompilerParams(
            collective_id=0, has_side_effects=True, vmem_limit_bytes=60 * 1024 * 1024
        ),
        cost_estimate=pl.CostEstimate(
            flops=2 * tok * width * width * zs + 12 * tok * tok * width,
            bytes_accessed=16 * 1024 * 1024,
            transcendentals=0,
        ),
    )(queries, keys, values, out_grad, slices)


def solution(mesh):
    placed = (
        P("seq", "head"),
        P("seq", "head"),
        P("seq", "head"),
        P("seq", "head"),
        P("head", None),
    )
    return jax.shard_map(
        on_device,
        mesh=mesh,
        in_specs=placed,
        out_specs=(P("seq", "head"), P("seq", "head"), P("seq", "head")),
        check_vma=False,
    )
```

```python
import functools
import math

import jax
import jax.numpy as jnp
from jax import lax
from jax.experimental import pallas as pl
from jax.experimental.pallas import tpu as pltpu
from jax.sharding import PartitionSpec as P

HD = 128
CH = 64
BLK = 256
AT2 = 13
AT3 = 24
LANES = 8
BF = jnp.bfloat16
F32 = jnp.float32
MESH = pl.DeviceIdType.MESH


def mm(a, b, dims):
    return lax.dot_general(a, b, (dims, ((), ())), preferred_element_type=F32)


NN = ((1,), (0,))
NT = ((1,), (1,))
TN = ((0,), (0,))


def kernel(
    factor, zs, rows_n, heads,
    q_hbm, k_hbm, v_hbm, x_hbm, w_hbm,
    res,
    q, k, v, w, xown, xq, gout, g, kacc, vacc, kst, qst, qst_b,
    pre, suf, in1, in2, tot, out3,
    load_sem, zsend, zrecv, fsend, frecv, wsend, wrecv, asend, arecv, bsend, brecv, dsend, drecv, csend, crecv, osend, orecv, s1, r1, s2, r2, s3, r3,
):
    qg, kg, vg = res.at[0], res.at[1], res.at[2]
    tok = q.shape[0]
    quarter = tok // 4
    subs = quarter // CH
    z = lax.axis_index("head")
    seq = lax.axis_index("seq")
    lane = lax.rem(seq, LANES)
    row = seq // LANES
    y, x, c = row, lane // 2, lax.rem(lane, 2)
    pair = z // 2
    side = 2 * lax.rem(z, 2) - 1

    def layer(n):
        return lax.rem(z + zs + n * side, zs)

    def seq_of(r, e):
        return r * LANES + e

    mine = pl.ds(pl.multiple_of(pair * quarter, quarter), quarter)
    loads = [
        pltpu.make_async_copy(x_hbm, xown, load_sem.at[0]),
        pltpu.make_async_copy(k_hbm, k, load_sem.at[1]),
        pltpu.make_async_copy(v_hbm, v, load_sem.at[2]),
        pltpu.make_async_copy(x_hbm.at[mine, :], xq.at[z], load_sem.at[3]),
        pltpu.make_async_copy(w_hbm, w.at[0], load_sem.at[4]),
        pltpu.make_async_copy(q_hbm, q, load_sem.at[5]),
    ]
    for cp in loads:
        cp.start()

    barrier = pltpu.get_barrier_semaphore()
    for n in (1, -1, 2, -2, 3):
        pl.semaphore_signal(barrier, inc=1, device_id={"head": layer(n)}, device_id_type=MESH)
    for d in range(1, LANES):
        pl.semaphore_signal(
            barrier, inc=1, device_id={"seq": seq_of(row, lax.rem(lane + d, LANES))}, device_id_type=MESH
        )
    for d in range(1, rows_n):
        pl.semaphore_signal(
            barrier, inc=1, device_id={"seq": seq_of(lax.rem(row + d, rows_n), lane)}, device_id_type=MESH
        )
    pl.semaphore_wait(barrier, 5 + (LANES - 1) + (rows_n - 1))

    def remote(ref, dst, send_sem, recv_sem, to):
        return pltpu.make_async_remote_copy(
            src_ref=ref, dst_ref=dst, send_sem=send_sem, recv_sem=recv_sem, device_id=to, device_id_type=MESH
        )

    def x_first(i, n):
        to = layer((1, -2, 3, -1)[i])
        rows = pl.ds(pl.multiple_of(to // 2 * quarter + n * CH, CH), CH)
        return remote(
            xown.at[rows, :], xq.at[z, pl.ds(n * CH, CH), :], zsend.at[i, n], zrecv.at[i, n], {"head": to}
        )

    def x_relay(i, n):
        piece = xq.at[layer(i + 1), pl.ds(n * CH, CH), :]
        return remote(piece, piece, fsend.at[i, n], frecv.at[i, n], {"head": layer(-1)})

    def w_z(b):
        return remote(
            w_hbm.at[c, y, x], w.at[b, c, y, x], wsend.at[b - 1], wrecv.at[b - 1], {"head": layer((1, -2, 3)[b - 1])}
        )

    half = x_hbm.shape[1] * zs // 2

    def w_first(b, part, d):
        piece = w.at[b, c, y, x, :, pl.ds(part * half, half)]
        to = seq_of(y, lax.rem(lane + 2 * d, LANES)) if part == 0 else seq_of(lax.rem(y + d, rows_n), lane)
        return remote(piece, piece, asend.at[b - 1, part, d - 1], arecv.at[b - 1, part, d - 1], {"seq": to})

    def w_line(b, part, n, cols):
        if part == 0:
            return w.at[b, c, lax.rem(y + n, rows_n), :, :, cols]
        return w.at[b, c, :, lax.rem(x + n, LANES // 2), :, cols]

    def w_next(part, n):
        if part == 0:
            return {"seq": seq_of(lax.rem(y + n, rows_n), lane)}
        return {"seq": seq_of(y, lax.rem(lane + 2 * n, LANES))}

    def w_second(b, part, way):
        piece = w_line(b, part, 0, pl.ds(part * half, half))
        return remote(
            piece, piece, bsend.at[b - 1, part, way], brecv.at[b - 1, part, way], w_next(part, (1, 3)[way])
        )

    def w_third(b, part, way):
        piece = w_line(b, part, (3, 1)[way], pl.ds(part * half + way * (half // 2), half // 2))
        return remote(
            piece, piece, dsend.at[b - 1, part, way], drecv.at[b - 1, part, way], w_next(part, (1, 3)[way])
        )

    def w_core(b, part, n):
        piece = w_line(b, part, n, pl.ds(part * half, half))
        return remote(
            piece, piece, csend.at[b - 1, part, n], crecv.at[b - 1, part, n], {"seq": seq_of(y, 2 * x + 1 - c)}
        )

    span = x_hbm.shape[1] // 2

    def of_core(core):
        return pl.ds(pl.multiple_of(core * span, span), span)

    def g_back(b, i):
        core = lax.rem(c + i, 2)
        return remote(
            gout.at[b - 1, :, of_core(core)], g.at[mine, of_core(core)], osend.at[b - 1, i], orecv.at[b - 1, i],
            {"head": layer(b)},
        )

    near = [(part, n) for part in range(2) for n in (0, 1, 3)]
    far = [(part, 2) for part in range(2)]
    ring3 = [(part, d) for part in range(2) for d in range(1, rows_n)]
    ways = [(part, way) for part in range(2) for way in range(2)]

    def start(make, b, keys):
        for key in keys:
            make(b, *key).start()

    def wait(make, b, keys):
        for key in keys:
            make(b, *key).wait_recv()

    def x_send(n):
        for i in (2, 1, 0, 3):
            x_first(i, n).start()

    def x_pass(n):
        for i in range(3):
            x_first(i, n).wait_recv()
            x_relay(i, n).start()

    sl = heads * HD // LANES

    def ex1(which, st, d):
        to = lax.rem(lane + d, LANES)
        return pltpu.make_async_remote_copy(
            src_ref=st.at[pl.ds(pl.multiple_of(to * sl, sl), sl), :],
            dst_ref=in1.at[which, lane],
            send_sem=s1.at[which, d],
            recv_sem=r1.at[which, d],
            device_id={"seq": seq_of(row, to)},
            device_id_type=MESH,
        )

    def ex2(which, d):
        return pltpu.make_async_remote_copy(
            src_ref=tot.at[which],
            dst_ref=in2.at[which, row],
            send_sem=s2.at[which, d],
            recv_sem=r2.at[which, d],
            device_id={"seq": seq_of(lax.rem(row + d, rows_n), lane)},
            device_id_type=MESH,
        )

    def ex3(which, fin, d):
        to = lax.rem(lane + d, LANES)
        return pltpu.make_async_remote_copy(
            src_ref=out3.at[which, to],
            dst_ref=fin.at[pl.ds(pl.multiple_of(lane * sl, sl), sl), :],
            send_sem=s3.at[which, d],
            recv_sem=r3.at[which, d],
            device_id={"seq": seq_of(row, to)},
            device_id_type=MESH,
        )

    def phase1(which, st):
        for d in range(1, LANES):
            ex1(which, st, d).start()
        in1[which, lane] = st[pl.ds(pl.multiple_of(lane * sl, sl), sl), :]

    def phase2(which, st):
        for d in range(1, LANES):
            ex1(which, st, d).wait_recv()
        total = in1[which, 0].astype(F32)
        for e in range(1, LANES):
            total = total + in1[which, e].astype(F32)
        tot[which] = total
        for d in range(1, rows_n):
            ex2(which, d).start()

    def phase3(which, fin):
        for d in range(1, rows_n):
            ex2(which, d).wait_recv()
        in2[which, row] = jnp.zeros((sl, HD), F32)
        run = jnp.zeros((sl, HD), F32)
        for r in range(rows_n):
            keep = (r < row) if which == 0 else (r > row)
            run = run + jnp.where(keep, in2[which, r], 0.0)
        for e in range(LANES) if which == 0 else reversed(range(LANES)):
            out3[which, e] = run.astype(BF)
            run = run + in1[which, e].astype(F32)
        for d in range(1, LANES):
            ex3(which, fin, d).start()
        fin[pl.ds(pl.multiple_of(lane * sl, sl), sl), :] = out3[which, lane]

    def phase4(which, fin):
        for d in range(1, LANES):
            ex3(which, fin, d).wait_recv()

    def col(h):
        return pl.ds(h * HD, HD)

    def product(b, core):
        xs = jnp.concatenate([xq[i] for i in range(zs)], axis=1)
        wb = w[b, core].reshape(span, x_hbm.shape[1] * zs)
        return mm(xs, wb, NT).astype(BF)

    def g_part(b, i):
        core = lax.rem(c + i, 2)
        if b == 0:
            g[mine, of_core(core)] = product(b, core)
        else:
            gout[b - 1, :, of_core(core)] = product(b, core)
            g_back(b, i).start()

    def add_state(rows, core):
        for i in range(heads // 2):
            here = pl.ds(pl.multiple_of(core * span + i * HD, HD), HD)
            qst[here, :] += mm(q[rows, here], g[rows, here], TN)

    def head_parts(h):
        causal = lax.broadcasted_iota(jnp.int32, (BLK, BLK), 0) >= lax.broadcasted_iota(
            jnp.int32, (BLK, BLK), 1
        )
        causal_t = lax.broadcasted_iota(jnp.int32, (BLK, BLK), 1) >= lax.broadcasted_iota(
            jnp.int32, (BLK, BLK), 0
        )

        def masked(a):
            diag = jnp.where(causal_t, a[:, :BLK], 0.0)
            if a.shape[1] > BLK:
                diag = jnp.concatenate([diag, a[:, BLK:]], axis=1)
            return diag.astype(BF)

        def kv_part(s0):
            rows, here = pl.ds(s0, tok - s0), pl.ds(s0, BLK)
            sct = masked(mm(v[here, col(h)], g[rows, col(h)], NT))
            kacc[here, col(h)] = mm(sct, q[rows, col(h)], NN)
            at = masked(mm(k[here, col(h)], q[rows, col(h)], NT))
            vacc[here, col(h)] = mm(at, g[rows, col(h)], NN)

        def q_part(r0):
            rows, past = pl.ds(r0, BLK), pl.ds(0, r0 + BLK)
            a = mm(g[rows, col(h)], v[past, col(h)], NT)
            diag = jnp.where(causal, a[:, r0:], 0.0)
            if r0:
                diag = jnp.concatenate([a[:, :r0], diag], axis=1)
            out = mm(diag.astype(BF), k[past, col(h)], NN) + mm(g[rows, col(h)], pre[col(h), :], NT)
            qg[rows, col(h)] = (factor * out).astype(BF)

        parts = [functools.partial(kv_part, s0) for s0 in range(0, tok, BLK)]
        return parts + [functools.partial(q_part, r0) for r0 in range(0, tok, BLK)]

    for b in (3, 2, 1):
        w_z(b).start()
    loads[0].wait()
    x_send(0)
    loads[1].wait()
    loads[2].wait()
    for h in range(heads):
        kst[col(h), :] = mm(k[:, col(h)], v[:, col(h)], TN).astype(BF)
    phase1(0, kst)
    qst[...] = jnp.zeros_like(qst)
    for b in (3, 2, 1):
        w_z(b).wait_recv()
        start(w_first, b, ring3)
        x_send(4 - b)
    wait(w_first, 3, ring3)
    start(w_second, 3, ways)
    x_pass(0)
    phase2(0, kst)
    wait(w_first, 2, ring3)
    wait(w_first, 1, ring3)
    x_pass(1)
    phase3(0, pre)
    wait(w_second, 3, ways)
    start(w_third, 3, ways)
    start(w_second, 2, ways)
    start(w_core, 3, near)
    x_pass(2)
    phase4(0, pre)
    wait(w_third, 3, ways)
    start(w_core, 3, far)
    wait(w_second, 2, ways)
    start(w_third, 2, ways)
    start(w_second, 1, ways)
    start(w_core, 2, near)
    x_pass(3)
    for n in range(subs):
        x_first(3, n).wait_recv()
        for i in range(3):
            x_relay(i, n).wait_recv()
    for cp in loads[3:]:
        cp.wait()
    g_part(3, 0)
    wait(w_core, 3, near + far)
    g_part(3, 1)
    wait(w_third, 2, ways)
    start(w_core, 2, far)
    g_part(2, 0)
    wait(w_second, 1, ways)
    start(w_third, 1, ways)
    start(w_core, 1, near)
    wait(w_core, 2, near + far)
    g_part(2, 1)
    g_part(0, 0)
    g_part(0, 1)
    add_state(mine, 0)
    add_state(mine, 1)
    wait(w_third, 1, ways)
    start(w_core, 1, far)
    g_part(1, 0)
    wait(w_core, 1, near + far)
    g_part(1, 1)
    for b in (3, 2, 1):
        rows = pl.ds(pl.multiple_of(layer((1, -2, 3)[b - 1]) // 2 * quarter, quarter), quarter)
        for i in range(2):
            g_back(b, i).wait_recv()
            add_state(rows, lax.rem(c + i, 2))
    qst_b[...] = qst[...].astype(BF)
    phase1(1, qst_b)
    for i, part in enumerate(sum([head_parts(h) for h in range(heads)], [])):
        if i == AT2:
            phase2(1, qst_b)
        if i == AT3:
            phase3(1, suf)
        part()
    phase4(1, suf)
    for h in range(heads):
        sh = suf[col(h), :]
        kg[:, col(h)] = (factor * (kacc[:, col(h)] + mm(v[:, col(h)], sh, NT))).astype(BF)
        vg[:, col(h)] = (factor * (vacc[:, col(h)] + mm(k[:, col(h)], sh, NN))).astype(BF)

    for n in range(subs):
        for i in range(4):
            x_first(i, n).wait_send()
        for i in range(3):
            x_relay(i, n).wait_send()
    for b in range(1, 4):
        w_z(b).wait_send()
        for key in ring3:
            w_first(b, *key).wait_send()
        for key in ways:
            w_second(b, *key).wait_send()
            w_third(b, *key).wait_send()
        for key in near + far:
            w_core(b, *key).wait_send()
        for i in range(2):
            g_back(b, i).wait_send()
    for which, st, fin in ((0, kst, pre), (1, qst_b, suf)):
        for d in range(1, LANES):
            ex1(which, st, d).wait_send()
            ex3(which, fin, d).wait_send()
        for d in range(1, rows_n):
            ex2(which, d).wait_send()


def on_device(queries, keys, values, out_grad, out_weight):
    tok, width = queries.shape
    zs = lax.axis_size("head")
    seqs = lax.axis_size("seq")
    heads = width // HD
    rows_n = seqs // LANES
    subs = tok // 4 // CH
    sl = heads * HD // LANES
    factor = 1.0 / math.sqrt(HD * tok * seqs)
    out = pltpu.VMEM((3, tok, width), BF)
    slices = out_weight.reshape(2, rows_n, LANES // 2, width // seqs, width * zs)
    dma = pltpu.SemaphoreType.DMA
    big = pl.pallas_call(
        functools.partial(kernel, factor, zs, rows_n, heads),
        out_shape=out,
        in_specs=[pl.BlockSpec(memory_space=pltpu.HBM)] * 5,
        out_specs=pl.BlockSpec(memory_space=pltpu.VMEM),
        scratch_shapes=[
            pltpu.VMEM((tok, width), BF),
            pltpu.VMEM((tok, width), BF),
            pltpu.VMEM((tok, width), BF),
            pltpu.VMEM((4, 2, rows_n, LANES // 2, width // seqs, width * zs), BF),
            pltpu.VMEM((tok, width), BF),
            pltpu.VMEM((zs, tok // 4, width), BF),
            pltpu.VMEM((3, tok // 4, width), BF),
            pltpu.VMEM((tok, width), BF),
            pltpu.VMEM((tok, width), F32),
            pltpu.VMEM((tok, width), F32),
            pltpu.VMEM((width, HD), BF),
            pltpu.VMEM((width, HD), F32),
            pltpu.VMEM((width, HD), BF),
            pltpu.VMEM((width, HD), BF),
            pltpu.VMEM((width, HD), BF),
            pltpu.VMEM((2, LANES, sl, HD), BF),
            pltpu.VMEM((2, rows_n, sl, HD), F32),
            pltpu.VMEM((2, sl, HD), F32),
            pltpu.VMEM((2, LANES, sl, HD), BF),
            dma((6,)),
            dma((4, subs)),
            dma((4, subs)),
            dma((3, subs)),
            dma((3, subs)),
            dma((3,)),
            dma((3,)),
            dma((3, 2, rows_n - 1)),
            dma((3, 2, rows_n - 1)),
            dma((3, 2, 2)),
            dma((3, 2, 2)),
            dma((3, 2, 2)),
            dma((3, 2, 2)),
            dma((3, 2, rows_n)),
            dma((3, 2, rows_n)),
            dma((3, 2)),
            dma((3, 2)),
            dma((2, LANES)),
            dma((2, LANES)),
            dma((2, rows_n)),
            dma((2, rows_n)),
            dma((2, LANES)),
            dma((2, LANES)),
        ],
        compiler_params=pltpu.CompilerParams(
            collective_id=0, has_side_effects=True, vmem_limit_bytes=60 * 1024 * 1024
        ),
        cost_estimate=pl.CostEstimate(
            flops=2 * tok * width * width * zs + 12 * tok * tok * width,
            bytes_accessed=16 * 1024 * 1024,
            transcendentals=0,
        ),
    )(queries, keys, values, out_grad, slices)
    return big[0], big[1], big[2]


def solution(mesh):
    placed = (
        P("seq", "head"),
        P("seq", "head"),
        P("seq", "head"),
        P("seq", "head"),
        P("head", None),
    )
    return jax.shard_map(
        on_device,
        mesh=mesh,
        in_specs=placed,
        out_specs=(P("seq", "head"), P("seq", "head"), P("seq", "head")),
        check_vma=False,
    )
```

```python
import functools
import math

import jax
import jax.numpy as jnp
from jax import lax
from jax.experimental import pallas as pl
from jax.experimental.pallas import tpu as pltpu
from jax.sharding import PartitionSpec as P

HD = 128
CH = 64
BLK = 256
AT2 = 13
AT3 = 24
LANES = 8
BF = jnp.bfloat16
F32 = jnp.float32
MESH = pl.DeviceIdType.MESH


def mm(a, b, dims):
    return lax.dot_general(a, b, (dims, ((), ())), preferred_element_type=F32)


NN = ((1,), (0,))
NT = ((1,), (1,))
TN = ((0,), (0,))


def kernel(
    factor, zs, rows_n, heads,
    q_hbm, k_hbm, v_hbm, x_hbm, w_hbm,
    res,
    q, k, v, w, xown, xq, gout, g, kacc, vacc, kst, qst, qst_b,
    pre, suf, in1, in2, tot, out3,
    load_sem, zsend, zrecv, fsend, frecv, wsend, wrecv, asend, arecv, bsend, brecv, dsend, drecv, csend, crecv, osend, orecv, s1, r1, s2, r2, s3, r3,
):
    qg, kg, vg = res.at[0], res.at[1], res.at[2]
    tok = q.shape[0]
    quarter = tok // 4
    subs = quarter // CH
    z = lax.axis_index("head")
    seq = lax.axis_index("seq")
    lane = lax.rem(seq, LANES)
    row = seq // LANES
    y, x, c = row, lane // 2, lax.rem(lane, 2)
    pair = z // 2
    side = 2 * lax.rem(z, 2) - 1

    def layer(n):
        return lax.rem(z + zs + n * side, zs)

    def seq_of(r, e):
        return r * LANES + e

    mine = pl.ds(pl.multiple_of(pair * quarter, quarter), quarter)
    loads = [
        pltpu.make_async_copy(x_hbm, xown, load_sem.at[0]),
        pltpu.make_async_copy(k_hbm, k, load_sem.at[1]),
        pltpu.make_async_copy(v_hbm, v, load_sem.at[2]),
        pltpu.make_async_copy(x_hbm.at[mine, :], xq.at[z], load_sem.at[3]),
        pltpu.make_async_copy(w_hbm, w.at[0], load_sem.at[4]),
        pltpu.make_async_copy(q_hbm, q, load_sem.at[5]),
    ]
    for cp in loads:
        cp.start()

    barrier = pltpu.get_barrier_semaphore()
    for n in (1, -1, 2, -2, 3):
        pl.semaphore_signal(barrier, inc=1, device_id={"head": layer(n)}, device_id_type=MESH)
    for d in range(1, LANES):
        pl.semaphore_signal(
            barrier, inc=1, device_id={"seq": seq_of(row, lax.rem(lane + d, LANES))}, device_id_type=MESH
        )
    for d in range(1, rows_n):
        pl.semaphore_signal(
            barrier, inc=1, device_id={"seq": seq_of(lax.rem(row + d, rows_n), lane)}, device_id_type=MESH
        )
    pl.semaphore_wait(barrier, 5 + (LANES - 1) + (rows_n - 1))

    def remote(ref, dst, send_sem, recv_sem, to):
        return pltpu.make_async_remote_copy(
            src_ref=ref, dst_ref=dst, send_sem=send_sem, recv_sem=recv_sem, device_id=to, device_id_type=MESH
        )

    def x_first(i, n):
        to = layer((1, -2, 3, -1)[i])
        rows = pl.ds(pl.multiple_of(to // 2 * quarter + n * CH, CH), CH)
        return remote(
            xown.at[rows, :], xq.at[z, pl.ds(n * CH, CH), :], zsend.at[i, n], zrecv.at[i, n], {"head": to}
        )

    def x_relay(i, n):
        piece = xq.at[layer(i + 1), pl.ds(n * CH, CH), :]
        return remote(piece, piece, fsend.at[i, n], frecv.at[i, n], {"head": layer(-1)})

    def w_z(b):
        return remote(
            w_hbm.at[c, y, x], w.at[b, c, y, x], wsend.at[b - 1], wrecv.at[b - 1], {"head": layer((1, -2, 3)[b - 1])}
        )

    half = x_hbm.shape[1] * zs // 2

    def w_first(b, part, d):
        piece = w.at[b, c, y, x, :, pl.ds(part * half, half)]
        to = seq_of(y, lax.rem(lane + 2 * d, LANES)) if part == 0 else seq_of(lax.rem(y + d, rows_n), lane)
        return remote(piece, piece, asend.at[b - 1, part, d - 1], arecv.at[b - 1, part, d - 1], {"seq": to})

    def w_line(b, part, n, cols):
        if part == 0:
            return w.at[b, c, lax.rem(y + n, rows_n), :, :, cols]
        return w.at[b, c, :, lax.rem(x + n, LANES // 2), :, cols]

    def w_next(part, n):
        if part == 0:
            return {"seq": seq_of(lax.rem(y + n, rows_n), lane)}
        return {"seq": seq_of(y, lax.rem(lane + 2 * n, LANES))}

    def w_second(b, part, way):
        piece = w_line(b, part, 0, pl.ds(part * half, half))
        return remote(
            piece, piece, bsend.at[b - 1, part, way], brecv.at[b - 1, part, way], w_next(part, (1, 3)[way])
        )

    def w_third(b, part, way):
        piece = w_line(b, part, (3, 1)[way], pl.ds(part * half + way * (half // 2), half // 2))
        return remote(
            piece, piece, dsend.at[b - 1, part, way], drecv.at[b - 1, part, way], w_next(part, (1, 3)[way])
        )

    def w_core(b, part, n):
        piece = w_line(b, part, n, pl.ds(part * half, half))
        return remote(
            piece, piece, csend.at[b - 1, part, n], crecv.at[b - 1, part, n], {"seq": seq_of(y, 2 * x + 1 - c)}
        )

    span = x_hbm.shape[1] // 2

    def of_core(core):
        return pl.ds(pl.multiple_of(core * span, span), span)

    part_rows = quarter // 2

    def g_back(b, i, t):
        core = lax.rem(c + i, 2)
        rows = pl.ds(pl.multiple_of(pair * quarter + t * part_rows, part_rows), part_rows)
        return remote(
            gout.at[b - 1, pl.ds(t * part_rows, part_rows), of_core(core)], g.at[rows, of_core(core)],
            osend.at[b - 1, i, t], orecv.at[b - 1, i, t], {"head": layer(b)},
        )

    near = [(part, n) for part in range(2) for n in (0, 1, 3)]
    far = [(part, 2) for part in range(2)]
    ring3 = [(part, d) for part in range(2) for d in range(1, rows_n)]
    ways = [(part, way) for part in range(2) for way in range(2)]

    def start(make, b, keys):
        for key in keys:
            make(b, *key).start()

    def wait(make, b, keys):
        for key in keys:
            make(b, *key).wait_recv()

    def x_send(n):
        for i in (2, 1, 0, 3):
            x_first(i, n).start()

    def x_pass(n):
        for i in range(3):
            x_first(i, n).wait_recv()
            x_relay(i, n).start()

    sl = heads * HD // LANES

    def ex1(which, st, d):
        to = lax.rem(lane + d, LANES)
        return pltpu.make_async_remote_copy(
            src_ref=st.at[pl.ds(pl.multiple_of(to * sl, sl), sl), :],
            dst_ref=in1.at[which, lane],
            send_sem=s1.at[which, d],
            recv_sem=r1.at[which, d],
            device_id={"seq": seq_of(row, to)},
            device_id_type=MESH,
        )

    def ex2(which, d):
        return pltpu.make_async_remote_copy(
            src_ref=tot.at[which],
            dst_ref=in2.at[which, row],
            send_sem=s2.at[which, d],
            recv_sem=r2.at[which, d],
            device_id={"seq": seq_of(lax.rem(row + d, rows_n), lane)},
            device_id_type=MESH,
        )

    def ex3(which, fin, d):
        to = lax.rem(lane + d, LANES)
        return pltpu.make_async_remote_copy(
            src_ref=out3.at[which, to],
            dst_ref=fin.at[pl.ds(pl.multiple_of(lane * sl, sl), sl), :],
            send_sem=s3.at[which, d],
            recv_sem=r3.at[which, d],
            device_id={"seq": seq_of(row, to)},
            device_id_type=MESH,
        )

    def phase1(which, st):
        for d in range(1, LANES):
            ex1(which, st, d).start()
        in1[which, lane] = st[pl.ds(pl.multiple_of(lane * sl, sl), sl), :]

    def phase2(which, st):
        for d in range(1, LANES):
            ex1(which, st, d).wait_recv()
        total = in1[which, 0].astype(F32)
        for e in range(1, LANES):
            total = total + in1[which, e].astype(F32)
        tot[which] = total
        for d in range(1, rows_n):
            ex2(which, d).start()

    def phase3(which, fin):
        for d in range(1, rows_n):
            ex2(which, d).wait_recv()
        in2[which, row] = jnp.zeros((sl, HD), F32)
        run = jnp.zeros((sl, HD), F32)
        for r in range(rows_n):
            keep = (r < row) if which == 0 else (r > row)
            run = run + jnp.where(keep, in2[which, r], 0.0)
        for e in range(LANES) if which == 0 else reversed(range(LANES)):
            out3[which, e] = run.astype(BF)
            run = run + in1[which, e].astype(F32)
        for d in range(1, LANES):
            ex3(which, fin, d).start()
        fin[pl.ds(pl.multiple_of(lane * sl, sl), sl), :] = out3[which, lane]

    def phase4(which, fin):
        for d in range(1, LANES):
            ex3(which, fin, d).wait_recv()

    def col(h):
        return pl.ds(h * HD, HD)

    def product(b, core, rows=slice(None)):
        xs = jnp.concatenate([xq[i, rows, :] for i in range(zs)], axis=1)
        wb = w[b, core].reshape(span, x_hbm.shape[1] * zs)
        return mm(xs, wb, NT).astype(BF)

    def g_part(b, i):
        core = lax.rem(c + i, 2)
        if b == 0:
            g[mine, of_core(core)] = product(b, core)
        else:
            gout[b - 1, :, of_core(core)] = product(b, core)
            for t in range(2):
                g_back(b, i, t).start()

    def g_half(b, i, t):
        core, rows = lax.rem(c + i, 2), pl.ds(t * part_rows, part_rows)
        gout[b - 1, rows, of_core(core)] = product(b, core, rows)
        g_back(b, i, t).start()

    def x_done(t):
        for n in range(t * subs // 2, (t + 1) * subs // 2):
            x_first(3, n).wait_recv()
            for i in range(3):
                x_relay(i, n).wait_recv()

    def add_state(rows, core):
        for i in range(heads // 2):
            here = pl.ds(pl.multiple_of(core * span + i * HD, HD), HD)
            qst[here, :] += mm(q[rows, here], g[rows, here], TN)

    def head_parts(h):
        causal = lax.broadcasted_iota(jnp.int32, (BLK, BLK), 0) >= lax.broadcasted_iota(
            jnp.int32, (BLK, BLK), 1
        )
        causal_t = lax.broadcasted_iota(jnp.int32, (BLK, BLK), 1) >= lax.broadcasted_iota(
            jnp.int32, (BLK, BLK), 0
        )

        def masked(a):
            diag = jnp.where(causal_t, a[:, :BLK], 0.0)
            if a.shape[1] > BLK:
                diag = jnp.concatenate([diag, a[:, BLK:]], axis=1)
            return diag.astype(BF)

        def kv_part(s0):
            rows, here = pl.ds(s0, tok - s0), pl.ds(s0, BLK)
            sct = masked(mm(v[here, col(h)], g[rows, col(h)], NT))
            kacc[here, col(h)] = mm(sct, q[rows, col(h)], NN)
            at = masked(mm(k[here, col(h)], q[rows, col(h)], NT))
            vacc[here, col(h)] = mm(at, g[rows, col(h)], NN)

        def q_part(r0):
            rows, past = pl.ds(r0, BLK), pl.ds(0, r0 + BLK)
            a = mm(g[rows, col(h)], v[past, col(h)], NT)
            diag = jnp.where(causal, a[:, r0:], 0.0)
            if r0:
                diag = jnp.concatenate([a[:, :r0], diag], axis=1)
            out = mm(diag.astype(BF), k[past, col(h)], NN) + mm(g[rows, col(h)], pre[col(h), :], NT)
            qg[rows, col(h)] = (factor * out).astype(BF)

        parts = [functools.partial(kv_part, s0) for s0 in range(0, tok, BLK)]
        return parts + [functools.partial(q_part, r0) for r0 in range(0, tok, BLK)]

    for b in (3, 2, 1):
        w_z(b).start()
    loads[0].wait()
    x_send(0)
    loads[1].wait()
    loads[2].wait()
    for h in range(heads):
        kst[col(h), :] = mm(k[:, col(h)], v[:, col(h)], TN).astype(BF)
    phase1(0, kst)
    qst[...] = jnp.zeros_like(qst)
    for b in (3, 2, 1):
        w_z(b).wait_recv()
        start(w_first, b, ring3)
        x_send(4 - b)
    wait(w_first, 3, ring3)
    start(w_second, 3, ways)
    x_pass(0)
    phase2(0, kst)
    wait(w_first, 2, ring3)
    wait(w_first, 1, ring3)
    x_pass(1)
    phase3(0, pre)
    wait(w_second, 3, ways)
    start(w_third, 3, ways)
    start(w_second, 2, ways)
    start(w_core, 3, near)
    x_pass(2)
    phase4(0, pre)
    wait(w_third, 3, ways)
    start(w_core, 3, far)
    wait(w_second, 2, ways)
    start(w_third, 2, ways)
    start(w_second, 1, ways)
    start(w_core, 2, near)
    x_pass(3)
    x_done(0)
    for cp in loads[3:]:
        cp.wait()
    wait(w_core, 3, near + far)
    g_half(3, 0, 0)
    g_half(3, 1, 0)
    x_done(1)
    g_half(3, 0, 1)
    g_half(3, 1, 1)
    wait(w_third, 2, ways)
    start(w_core, 2, far)
    g_part(2, 0)
    wait(w_second, 1, ways)
    start(w_third, 1, ways)
    start(w_core, 1, near)
    wait(w_core, 2, near + far)
    g_part(2, 1)
    g_part(0, 0)
    g_part(0, 1)
    add_state(mine, 0)
    add_state(mine, 1)
    wait(w_third, 1, ways)
    start(w_core, 1, far)
    g_part(1, 0)
    wait(w_core, 1, near + far)
    g_part(1, 1)
    for b in (3, 2, 1):
        rows = pl.ds(pl.multiple_of(layer((1, -2, 3)[b - 1]) // 2 * quarter, quarter), quarter)
        for i in range(2):
            g_back(b, i, 0).wait_recv()
            g_back(b, i, 1).wait_recv()
            add_state(rows, lax.rem(c + i, 2))
    qst_b[...] = qst[...].astype(BF)
    phase1(1, qst_b)
    for i, part in enumerate(sum([head_parts(h) for h in range(heads)], [])):
        if i == AT2:
            phase2(1, qst_b)
        if i == AT3:
            phase3(1, suf)
        part()
    for n in range(subs):
        for i in range(4):
            x_first(i, n).wait_send()
        for i in range(3):
            x_relay(i, n).wait_send()
    for b in range(1, 4):
        w_z(b).wait_send()
        for key in ring3:
            w_first(b, *key).wait_send()
        for key in ways:
            w_second(b, *key).wait_send()
            w_third(b, *key).wait_send()
        for key in near + far:
            w_core(b, *key).wait_send()
        for i in range(2):
            g_back(b, i, 0).wait_send()
            g_back(b, i, 1).wait_send()
    for which, st, fin in ((0, kst, pre), (1, qst_b, suf)):
        for d in range(1, LANES):
            ex1(which, st, d).wait_send()
            if which == 0:
                ex3(which, fin, d).wait_send()
        for d in range(1, rows_n):
            ex2(which, d).wait_send()
    phase4(1, suf)
    for h in range(heads):
        sh = suf[col(h), :]
        kg[:, col(h)] = (factor * (kacc[:, col(h)] + mm(v[:, col(h)], sh, NT))).astype(BF)
        vg[:, col(h)] = (factor * (vacc[:, col(h)] + mm(k[:, col(h)], sh, NN))).astype(BF)
    for d in range(1, LANES):
        ex3(1, suf, d).wait_send()


def on_device(queries, keys, values, out_grad, out_weight):
    tok, width = queries.shape
    zs = lax.axis_size("head")
    seqs = lax.axis_size("seq")
    heads = width // HD
    rows_n = seqs // LANES
    subs = tok // 4 // CH
    sl = heads * HD // LANES
    factor = 1.0 / math.sqrt(HD * tok * seqs)
    out = pltpu.VMEM((3, tok, width), BF)
    slices = out_weight.reshape(2, rows_n, LANES // 2, width // seqs, width * zs)
    dma = pltpu.SemaphoreType.DMA
    big = pl.pallas_call(
        functools.partial(kernel, factor, zs, rows_n, heads),
        out_shape=out,
        in_specs=[pl.BlockSpec(memory_space=pltpu.HBM)] * 5,
        out_specs=pl.BlockSpec(memory_space=pltpu.VMEM),
        scratch_shapes=[
            pltpu.VMEM((tok, width), BF),
            pltpu.VMEM((tok, width), BF),
            pltpu.VMEM((tok, width), BF),
            pltpu.VMEM((4, 2, rows_n, LANES // 2, width // seqs, width * zs), BF),
            pltpu.VMEM((tok, width), BF),
            pltpu.VMEM((zs, tok // 4, width), BF),
            pltpu.VMEM((3, tok // 4, width), BF),
            pltpu.VMEM((tok, width), BF),
            pltpu.VMEM((tok, width), F32),
            pltpu.VMEM((tok, width), F32),
            pltpu.VMEM((width, HD), BF),
            pltpu.VMEM((width, HD), F32),
            pltpu.VMEM((width, HD), BF),
            pltpu.VMEM((width, HD), BF),
            pltpu.VMEM((width, HD), BF),
            pltpu.VMEM((2, LANES, sl, HD), BF),
            pltpu.VMEM((2, rows_n, sl, HD), F32),
            pltpu.VMEM((2, sl, HD), F32),
            pltpu.VMEM((2, LANES, sl, HD), BF),
            dma((6,)),
            dma((4, subs)),
            dma((4, subs)),
            dma((3, subs)),
            dma((3, subs)),
            dma((3,)),
            dma((3,)),
            dma((3, 2, rows_n - 1)),
            dma((3, 2, rows_n - 1)),
            dma((3, 2, 2)),
            dma((3, 2, 2)),
            dma((3, 2, 2)),
            dma((3, 2, 2)),
            dma((3, 2, rows_n)),
            dma((3, 2, rows_n)),
            dma((3, 2, 2)),
            dma((3, 2, 2)),
            dma((2, LANES)),
            dma((2, LANES)),
            dma((2, rows_n)),
            dma((2, rows_n)),
            dma((2, LANES)),
            dma((2, LANES)),
        ],
        compiler_params=pltpu.CompilerParams(
            collective_id=0, has_side_effects=True, vmem_limit_bytes=60 * 1024 * 1024
        ),
        cost_estimate=pl.CostEstimate(
            flops=2 * tok * width * width * zs + 12 * tok * tok * width,
            bytes_accessed=16 * 1024 * 1024,
            transcendentals=0,
        ),
    )(queries, keys, values, out_grad, slices)
    return big[0], big[1], big[2]


def solution(mesh):
    placed = (
        P("seq", "head"),
        P("seq", "head"),
        P("seq", "head"),
        P("seq", "head"),
        P("head", None),
    )
    return jax.shard_map(
        on_device,
        mesh=mesh,
        in_specs=placed,
        out_specs=(P("seq", "head"), P("seq", "head"), P("seq", "head")),
        check_vma=False,
    )
```

```python
import functools
import math

import jax
import jax.numpy as jnp
from jax import lax
from jax.experimental import pallas as pl
from jax.experimental.pallas import tpu as pltpu
from jax.sharding import PartitionSpec as P

HD = 128
CH = 64
BLK = 256
AT2 = 10
AT3 = 20
LANES = 8
BF = jnp.bfloat16
F32 = jnp.float32
MESH = pl.DeviceIdType.MESH


def mm(a, b, dims):
    return lax.dot_general(a, b, (dims, ((), ())), preferred_element_type=F32)


NN = ((1,), (0,))
NT = ((1,), (1,))
TN = ((0,), (0,))


def kernel(
    factor, zs, rows_n, heads,
    q_hbm, k_hbm, v_hbm, x_hbm, w_hbm,
    res,
    q, k, v, w, xown, xq, gout, g, kacc, vacc, kst, qst, qst_b,
    pre, suf, in1, in2, tot, out3,
    load_sem, zsend, zrecv, fsend, frecv, wsend, wrecv, asend, arecv, bsend, brecv, dsend, drecv, csend, crecv, osend, orecv, s1, r1, s2, r2, s3, r3,
):
    qg, kg, vg = res.at[0], res.at[1], res.at[2]
    tok = q.shape[0]
    quarter = tok // 4
    subs = quarter // CH
    z = lax.axis_index("head")
    seq = lax.axis_index("seq")
    lane = lax.rem(seq, LANES)
    row = seq // LANES
    y, x, c = row, lane // 2, lax.rem(lane, 2)
    pair = z // 2
    side = 2 * lax.rem(z, 2) - 1

    def layer(n):
        return lax.rem(z + zs + n * side, zs)

    def seq_of(r, e):
        return r * LANES + e

    mine = pl.ds(pl.multiple_of(pair * quarter, quarter), quarter)
    loads = [
        pltpu.make_async_copy(x_hbm, xown, load_sem.at[0]),
        pltpu.make_async_copy(k_hbm, k, load_sem.at[1]),
        pltpu.make_async_copy(v_hbm, v, load_sem.at[2]),
        pltpu.make_async_copy(x_hbm.at[mine, :], xq.at[z], load_sem.at[3]),
        pltpu.make_async_copy(w_hbm, w.at[0], load_sem.at[4]),
        pltpu.make_async_copy(q_hbm, q, load_sem.at[5]),
    ]
    for cp in loads:
        cp.start()

    barrier = pltpu.get_barrier_semaphore()
    for n in (1, -1, 2, -2, 3):
        pl.semaphore_signal(barrier, inc=1, device_id={"head": layer(n)}, device_id_type=MESH)
    for d in range(1, LANES):
        pl.semaphore_signal(
            barrier, inc=1, device_id={"seq": seq_of(row, lax.rem(lane + d, LANES))}, device_id_type=MESH
        )
    for d in range(1, rows_n):
        pl.semaphore_signal(
            barrier, inc=1, device_id={"seq": seq_of(lax.rem(row + d, rows_n), lane)}, device_id_type=MESH
        )
    pl.semaphore_wait(barrier, 5 + (LANES - 1) + (rows_n - 1))

    def remote(ref, dst, send_sem, recv_sem, to):
        return pltpu.make_async_remote_copy(
            src_ref=ref, dst_ref=dst, send_sem=send_sem, recv_sem=recv_sem, device_id=to, device_id_type=MESH
        )

    def x_first(i, n):
        to = layer((1, -2, 3, -1)[i])
        rows = pl.ds(pl.multiple_of(to // 2 * quarter + n * CH, CH), CH)
        return remote(
            xown.at[rows, :], xq.at[z, pl.ds(n * CH, CH), :], zsend.at[i, n], zrecv.at[i, n], {"head": to}
        )

    def x_relay(i, n):
        piece = xq.at[layer(i + 1), pl.ds(n * CH, CH), :]
        return remote(piece, piece, fsend.at[i, n], frecv.at[i, n], {"head": layer(-1)})

    def w_z(b):
        src, to = (w.at[1, c, y, x], -2) if b == 3 else (w_hbm.at[c, y, x], (1, -2)[b - 1])
        return remote(src, w.at[b, c, y, x], wsend.at[b - 1], wrecv.at[b - 1], {"head": layer(to)})

    half = x_hbm.shape[1] * zs // 2

    def w_first(b, part, d):
        piece = w.at[b, c, y, x, :, pl.ds(part * half, half)]
        to = seq_of(y, lax.rem(lane + 2 * d, LANES)) if part == 0 else seq_of(lax.rem(y + d, rows_n), lane)
        return remote(piece, piece, asend.at[b - 1, part, d - 1], arecv.at[b - 1, part, d - 1], {"seq": to})

    def w_line(b, part, n, cols):
        if part == 0:
            return w.at[b, c, lax.rem(y + n, rows_n), :, :, cols]
        return w.at[b, c, :, lax.rem(x + n, LANES // 2), :, cols]

    def w_next(part, n):
        if part == 0:
            return {"seq": seq_of(lax.rem(y + n, rows_n), lane)}
        return {"seq": seq_of(y, lax.rem(lane + 2 * n, LANES))}

    def w_second(b, part, way):
        piece = w_line(b, part, 0, pl.ds(part * half, half))
        return remote(
            piece, piece, bsend.at[b - 1, part, way], brecv.at[b - 1, part, way], w_next(part, (1, 3)[way])
        )

    def w_third(b, part, way):
        piece = w_line(b, part, (3, 1)[way], pl.ds(part * half + way * (half // 2), half // 2))
        return remote(
            piece, piece, dsend.at[b - 1, part, way], drecv.at[b - 1, part, way], w_next(part, (1, 3)[way])
        )

    def w_core(b, part, n):
        piece = w_line(b, part, n, pl.ds(part * half, half))
        return remote(
            piece, piece, csend.at[b - 1, part, n], crecv.at[b - 1, part, n], {"seq": seq_of(y, 2 * x + 1 - c)}
        )

    span = x_hbm.shape[1] // 2

    def of_core(core):
        return pl.ds(pl.multiple_of(core * span, span), span)

    part_rows = quarter // 2

    def g_back(b, i, t):
        core = lax.rem(c + i, 2)
        rows = pl.ds(pl.multiple_of(pair * quarter + t * part_rows, part_rows), part_rows)
        return remote(
            gout.at[b - 1, pl.ds(t * part_rows, part_rows), of_core(core)], g.at[rows, of_core(core)],
            osend.at[b - 1, i, t], orecv.at[b - 1, i, t], {"head": layer(b)},
        )

    near = [(part, n) for part in range(2) for n in (0, 1, 3)]
    far = [(part, 2) for part in range(2)]
    ring3 = [(part, d) for part in range(2) for d in range(1, rows_n)]
    ways = [(part, way) for part in range(2) for way in range(2)]

    def start(make, b, keys):
        for key in keys:
            make(b, *key).start()

    def wait(make, b, keys):
        for key in keys:
            make(b, *key).wait_recv()

    def x_send(n):
        for i in (2, 1, 0, 3):
            x_first(i, n).start()

    def x_pass(n):
        for i in range(3):
            x_first(i, n).wait_recv()
            x_relay(i, n).start()

    sl = heads * HD // LANES

    def ex1(which, st, d):
        to = lax.rem(lane + d, LANES)
        return pltpu.make_async_remote_copy(
            src_ref=st.at[pl.ds(pl.multiple_of(to * sl, sl), sl), :],
            dst_ref=in1.at[which, lane],
            send_sem=s1.at[which, d],
            recv_sem=r1.at[which, d],
            device_id={"seq": seq_of(row, to)},
            device_id_type=MESH,
        )

    def ex2(which, d):
        return pltpu.make_async_remote_copy(
            src_ref=tot.at[which],
            dst_ref=in2.at[which, row],
            send_sem=s2.at[which, d],
            recv_sem=r2.at[which, d],
            device_id={"seq": seq_of(lax.rem(row + d, rows_n), lane)},
            device_id_type=MESH,
        )

    def ex3(which, fin, d):
        to = lax.rem(lane + d, LANES)
        return pltpu.make_async_remote_copy(
            src_ref=out3.at[which, to],
            dst_ref=fin.at[pl.ds(pl.multiple_of(lane * sl, sl), sl), :],
            send_sem=s3.at[which, d],
            recv_sem=r3.at[which, d],
            device_id={"seq": seq_of(row, to)},
            device_id_type=MESH,
        )

    def phase1(which, st):
        for d in range(1, LANES):
            ex1(which, st, d).start()
        in1[which, lane] = st[pl.ds(pl.multiple_of(lane * sl, sl), sl), :]

    def phase2(which, st):
        for d in range(1, LANES):
            ex1(which, st, d).wait_recv()
        total = in1[which, 0].astype(F32)
        for e in range(1, LANES):
            total = total + in1[which, e].astype(F32)
        tot[which] = total
        for d in range(1, rows_n):
            ex2(which, d).start()

    def phase3(which, fin):
        for d in range(1, rows_n):
            ex2(which, d).wait_recv()
        in2[which, row] = jnp.zeros((sl, HD), F32)
        run = jnp.zeros((sl, HD), F32)
        for r in range(rows_n):
            keep = (r < row) if which == 0 else (r > row)
            run = run + jnp.where(keep, in2[which, r], 0.0)
        for e in range(LANES) if which == 0 else reversed(range(LANES)):
            out3[which, e] = run.astype(BF)
            run = run + in1[which, e].astype(F32)
        for d in range(1, LANES):
            ex3(which, fin, d).start()
        fin[pl.ds(pl.multiple_of(lane * sl, sl), sl), :] = out3[which, lane]

    def phase4(which, fin):
        for d in range(1, LANES):
            ex3(which, fin, d).wait_recv()

    def col(h):
        return pl.ds(h * HD, HD)

    def product(b, core, rows=slice(None)):
        xs = jnp.concatenate([xq[i, rows, :] for i in range(zs)], axis=1)
        wb = w[b, core].reshape(span, x_hbm.shape[1] * zs)
        return mm(xs, wb, NT).astype(BF)

    def g_part(b, i):
        core = lax.rem(c + i, 2)
        if b == 0:
            g[mine, of_core(core)] = product(b, core)
        else:
            gout[b - 1, :, of_core(core)] = product(b, core)
            for t in range(2):
                g_back(b, i, t).start()

    def g_half(b, i, t):
        core, rows = lax.rem(c + i, 2), pl.ds(t * part_rows, part_rows)
        gout[b - 1, rows, of_core(core)] = product(b, core, rows)
        g_back(b, i, t).start()

    def x_done(t):
        for n in range(t * subs // 2, (t + 1) * subs // 2):
            x_first(3, n).wait_recv()
            for i in range(3):
                x_relay(i, n).wait_recv()

    def add_state(rows, core):
        for i in range(heads // 2):
            here = pl.ds(pl.multiple_of(core * span + i * HD, HD), HD)
            qst[here, :] += mm(q[rows, here], g[rows, here], TN)

    def head_parts(h):
        causal = lax.broadcasted_iota(jnp.int32, (BLK, BLK), 0) >= lax.broadcasted_iota(
            jnp.int32, (BLK, BLK), 1
        )
        causal_t = lax.broadcasted_iota(jnp.int32, (BLK, BLK), 1) >= lax.broadcasted_iota(
            jnp.int32, (BLK, BLK), 0
        )

        def masked(a):
            diag = jnp.where(causal_t, a[:, :BLK], 0.0)
            if a.shape[1] > BLK:
                diag = jnp.concatenate([diag, a[:, BLK:]], axis=1)
            return diag.astype(BF)

        def kv_part(s0):
            rows, here = pl.ds(s0, tok - s0), pl.ds(s0, BLK)
            sct = masked(mm(v[here, col(h)], g[rows, col(h)], NT))
            kacc[here, col(h)] = mm(sct, q[rows, col(h)], NN)
            at = masked(mm(k[here, col(h)], q[rows, col(h)], NT))
            vacc[here, col(h)] = mm(at, g[rows, col(h)], NN)

        def q_part(r0):
            rows, past = pl.ds(r0, BLK), pl.ds(0, r0 + BLK)
            a = mm(g[rows, col(h)], v[past, col(h)], NT)
            diag = jnp.where(causal, a[:, r0:], 0.0)
            if r0:
                diag = jnp.concatenate([a[:, :r0], diag], axis=1)
            out = mm(diag.astype(BF), k[past, col(h)], NN) + mm(g[rows, col(h)], pre[col(h), :], NT)
            qg[rows, col(h)] = (factor * out).astype(BF)

        parts = [functools.partial(kv_part, s0) for s0 in range(0, tok, BLK)]
        return parts + [functools.partial(q_part, r0) for r0 in range(0, tok, BLK)]

    w_z(1).start()
    w_z(2).start()
    loads[0].wait()
    x_send(0)
    loads[1].wait()
    loads[2].wait()
    for h in range(heads):
        kst[col(h), :] = mm(k[:, col(h)], v[:, col(h)], TN).astype(BF)
    phase1(0, kst)
    qst[...] = jnp.zeros_like(qst)
    for b in (1, 2, 3):
        w_z(b).wait_recv()
        if b == 1:
            w_z(3).start()
        start(w_first, b, ring3)
        x_send(b)
    wait(w_first, 3, ring3)
    start(w_second, 3, ways)
    x_pass(0)
    wait(w_first, 2, ring3)
    wait(w_first, 1, ring3)
    x_pass(1)
    phase2(0, kst)
    wait(w_second, 3, ways)
    start(w_third, 3, ways)
    start(w_second, 2, ways)
    start(w_core, 3, near)
    x_pass(2)
    phase3(0, pre)
    wait(w_third, 3, ways)
    start(w_core, 3, far)
    wait(w_second, 2, ways)
    start(w_third, 2, ways)
    start(w_second, 1, ways)
    start(w_core, 2, near)
    x_pass(3)
    x_done(0)
    for cp in loads[3:]:
        cp.wait()
    wait(w_core, 3, near + far)
    g_half(3, 0, 0)
    g_half(3, 1, 0)
    phase4(0, pre)
    x_done(1)
    g_half(3, 0, 1)
    g_half(3, 1, 1)
    wait(w_third, 2, ways)
    start(w_core, 2, far)
    g_part(2, 0)
    wait(w_second, 1, ways)
    start(w_third, 1, ways)
    start(w_core, 1, near)
    wait(w_core, 2, near + far)
    g_part(2, 1)
    g_part(0, 0)
    g_part(0, 1)
    add_state(mine, 0)
    add_state(mine, 1)
    wait(w_third, 1, ways)
    start(w_core, 1, far)
    g_part(1, 0)
    wait(w_core, 1, near + far)
    g_part(1, 1)
    for b in (3, 2, 1):
        rows = pl.ds(pl.multiple_of(layer((1, -2, 3)[b - 1]) // 2 * quarter, quarter), quarter)
        for i in range(2):
            g_back(b, i, 0).wait_recv()
            g_back(b, i, 1).wait_recv()
            add_state(rows, lax.rem(c + i, 2))
    qst_b[...] = qst[...].astype(BF)
    phase1(1, qst_b)
    for i, part in enumerate(sum([head_parts(h) for h in range(heads)], [])):
        if i == AT2:
            phase2(1, qst_b)
        if i == AT3:
            phase3(1, suf)
        part()
    for n in range(subs):
        for i in range(4):
            x_first(i, n).wait_send()
        for i in range(3):
            x_relay(i, n).wait_send()
    for b in range(1, 4):
        w_z(b).wait_send()
        for key in ring3:
            w_first(b, *key).wait_send()
        for key in ways:
            w_second(b, *key).wait_send()
            w_third(b, *key).wait_send()
        for key in near + far:
            w_core(b, *key).wait_send()
        for i in range(2):
            g_back(b, i, 0).wait_send()
            g_back(b, i, 1).wait_send()
    for which, st, fin in ((0, kst, pre), (1, qst_b, suf)):
        for d in range(1, LANES):
            ex1(which, st, d).wait_send()
            if which == 0:
                ex3(which, fin, d).wait_send()
        for d in range(1, rows_n):
            ex2(which, d).wait_send()
    phase4(1, suf)
    for h in range(heads):
        sh = suf[col(h), :]
        kg[:, col(h)] = (factor * (kacc[:, col(h)] + mm(v[:, col(h)], sh, NT))).astype(BF)
        vg[:, col(h)] = (factor * (vacc[:, col(h)] + mm(k[:, col(h)], sh, NN))).astype(BF)
    for d in range(1, LANES):
        ex3(1, suf, d).wait_send()


def on_device(queries, keys, values, out_grad, out_weight):
    tok, width = queries.shape
    zs = lax.axis_size("head")
    seqs = lax.axis_size("seq")
    heads = width // HD
    rows_n = seqs // LANES
    subs = tok // 4 // CH
    sl = heads * HD // LANES
    factor = 1.0 / math.sqrt(HD * tok * seqs)
    out = pltpu.VMEM((3, tok, width), BF)
    slices = out_weight.reshape(2, rows_n, LANES // 2, width // seqs, width * zs)
    dma = pltpu.SemaphoreType.DMA
    big = pl.pallas_call(
        functools.partial(kernel, factor, zs, rows_n, heads),
        out_shape=out,
        in_specs=[pl.BlockSpec(memory_space=pltpu.HBM)] * 5,
        out_specs=pl.BlockSpec(memory_space=pltpu.VMEM),
        scratch_shapes=[
            pltpu.VMEM((tok, width), BF),
            pltpu.VMEM((tok, width), BF),
            pltpu.VMEM((tok, width), BF),
            pltpu.VMEM((4, 2, rows_n, LANES // 2, width // seqs, width * zs), BF),
            pltpu.VMEM((tok, width), BF),
            pltpu.VMEM((zs, tok // 4, width), BF),
            pltpu.VMEM((3, tok // 4, width), BF),
            pltpu.VMEM((tok, width), BF),
            pltpu.VMEM((tok, width), F32),
            pltpu.VMEM((tok, width), F32),
            pltpu.VMEM((width, HD), BF),
            pltpu.VMEM((width, HD), F32),
            pltpu.VMEM((width, HD), BF),
            pltpu.VMEM((width, HD), BF),
            pltpu.VMEM((width, HD), BF),
            pltpu.VMEM((2, LANES, sl, HD), BF),
            pltpu.VMEM((2, rows_n, sl, HD), F32),
            pltpu.VMEM((2, sl, HD), F32),
            pltpu.VMEM((2, LANES, sl, HD), BF),
            dma((6,)),
            dma((4, subs)),
            dma((4, subs)),
            dma((3, subs)),
            dma((3, subs)),
            dma((3,)),
            dma((3,)),
            dma((3, 2, rows_n - 1)),
            dma((3, 2, rows_n - 1)),
            dma((3, 2, 2)),
            dma((3, 2, 2)),
            dma((3, 2, 2)),
            dma((3, 2, 2)),
            dma((3, 2, rows_n)),
            dma((3, 2, rows_n)),
            dma((3, 2, 2)),
            dma((3, 2, 2)),
            dma((2, LANES)),
            dma((2, LANES)),
            dma((2, rows_n)),
            dma((2, rows_n)),
            dma((2, LANES)),
            dma((2, LANES)),
        ],
        compiler_params=pltpu.CompilerParams(
            collective_id=0, has_side_effects=True, vmem_limit_bytes=60 * 1024 * 1024
        ),
        cost_estimate=pl.CostEstimate(
            flops=2 * tok * width * width * zs + 12 * tok * tok * width,
            bytes_accessed=16 * 1024 * 1024,
            transcendentals=0,
        ),
    )(queries, keys, values, out_grad, slices)
    return big[0], big[1], big[2]


def solution(mesh):
    placed = (
        P("seq", "head"),
        P("seq", "head"),
        P("seq", "head"),
        P("seq", "head"),
        P("head", None),
    )
    return jax.shard_map(
        on_device,
        mesh=mesh,
        in_specs=placed,
        out_specs=(P("seq", "head"), P("seq", "head"), P("seq", "head")),
        check_vma=False,
    )
```
